32 devices in a mesh: groups: 2 (over y), aux: 4 (over z), orb: 4 (over x, core).
Axes of the slice: x: 2, y: 2, z: 4, core: 2. Of those that a mesh axis runs over, the one named last changes fastest.
Arguments:
- tiles: bfloat16 [512, 128, 128], P(('groups', 'aux')), parts along dimension 0, may hold values from -0.25 to 0.25
- slot_aux: int32 [8, 64], P('groups'), parts along dimension 0, may hold values from 0 to 31
- slot_basis: int32 [8, 64], P('groups'), parts along dimension 0, may hold values from 0 to 239, as said below
- slot_count: int32 [8], P('groups'), parts along dimension 0, may hold values from 8 to 64
- orbitals: bfloat16 [61440, 2048], P(('groups', 'aux'), 'orb'), parts along dimension 0, may hold values from -6 to 6
- fit_rows: bfloat16 [8192, 4096], P(('groups', 'aux')), parts along dimension 0, may hold values from -1 to 1
Outputs:
- exchange: float32 [4096, 2048], P(('groups', 'aux'), 'orb'), parts along dimension 0
The draws below stay inside these ranges and needn't reach their ends.
There are 2 independent parts, one for each index of `groups`. The reference program is written for one: setup_inputs(seed, part) draws one part's arguments, and reference() takes and returns one part's arrays. A program takes and returns all parts, laid end to end along the dimension named above; each array names one. Nothing has to cross between parts.
Inputs may be any that keep to these rules, and one draw needn't show every extreme that they name: `slot_basis`: within each row, the first slot_count entries never fall.
All inputs are finite; a program needn't handle non-finite values.
Results may differ from the reference program's by a relative error of at most 0.0031.
Values may be sent and summed in bfloat16 or wider, within the bound.
No kernel may reach another device: no remote copies, remote signals or barrier semaphores. Data moves between devices by JAX's collectives and lax.ppermute only.
A program may use at most 192 MiB of HBM per device.

```python
import jax
import jax.numpy as jnp
from jax import lax

NBAS = 30720
NAUX = 4096
NOCC = 2048
TILE = 128
SLOTS = 64
N_AUX = 4


def slot_tables(key):
    shifts = jax.random.randint(jax.random.fold_in(key, 11), (N_AUX,), 0, 4).astype(jnp.int32)
    halved = jnp.right_shift(jnp.full((N_AUX,), SLOTS, jnp.int32), shifts)
    heaviest = jax.random.randint(jax.random.fold_in(key, 12), (), 0, N_AUX)
    counts = jnp.where(jnp.arange(N_AUX) == heaviest, SLOTS, halved).astype(jnp.int32)
    per_device = NAUX // TILE // N_AUX
    own_block = jnp.arange(N_AUX)[:, None] * per_device + jax.random.randint(jax.random.fold_in(key, 13), (N_AUX, SLOTS), 0, per_device)
    anywhere = jax.random.randint(jax.random.fold_in(key, 14), (N_AUX, SLOTS), 0, NAUX // TILE)
    chooser = jax.random.randint(jax.random.fold_in(key, 15), (N_AUX, SLOTS), 0, 2)
    owners = jnp.where(chooser == 0, own_block, anywhere).astype(jnp.int32)
    raw_basis = jax.random.randint(jax.random.fold_in(key, 16), (N_AUX, SLOTS), 0, NBAS // TILE)
    padding = (jnp.arange(SLOTS)[None, :] >= counts[:, None]).astype(jnp.int32)
    ordered = jnp.sort(raw_basis + NBAS // TILE * padding, axis=1)
    bases = (ordered % (NBAS // TILE)).astype(jnp.int32)
    return (owners, bases, counts)


def draw_slot_aux(key, part):
    return slot_tables(key)[0]


def draw_slot_basis(key, part):
    return slot_tables(key)[1]


def draw_slot_count(key, part):
    return slot_tables(key)[2]


def draw_orbitals(key, part):
    key = jax.random.fold_in(key, 3)
    noise = jnp.clip(jax.random.normal(key, (NBAS, NOCC), jnp.float32), -4.0, 4.0)
    return ((noise + jnp.roll(noise, 1, axis=1)) * 0.7071).astype(jnp.bfloat16)


def draw_fit_rows(key, part):
    key = jax.random.fold_in(key, 5)
    noise = jnp.clip(jax.random.normal(key, (NAUX, NAUX), jnp.float32), -4.0, 4.0)
    row_index = jnp.arange(NAUX)[:, None]
    col_index = jnp.arange(NAUX)[None, :]
    diagonal_part = (row_index == col_index).astype(jnp.float32)
    return ((diagonal_part + 0.5 * noise * NAUX ** (-0.5)) * NAUX ** (-0.5)).astype(jnp.bfloat16)


def level_of(stream_key, dims, cuts, least, largest):
    def one(dim, blocks):
        heights = jax.random.uniform(jax.random.fold_in(jax.random.fold_in(stream_key, 6), dim), (blocks,), jnp.float32, least / len(cuts), largest / len(cuts))
        return jnp.repeat(jnp.exp(heights), dims[dim] // blocks).reshape((-1,) + (1,) * (len(dims) - dim - 1))

    loudness = one(*cuts[0])
    for cut in cuts[1:]:
        loudness = loudness * one(*cut)
    return loudness


def gaussian(rng, shape, scale, most, split=(), kind=jnp.bfloat16):
    array = scale * jax.random.normal(rng, shape, jnp.float32)
    if split:
        array = array * level_of(rng, shape, split, -0.22, 0.18)
    return jnp.clip(array, -most, most).astype(kind)


def setup_inputs(seed: int = 0, part: int = 0) -> dict:
    keys = jax.random.split(jax.random.key(seed), 7)
    part_keys = jax.random.split(jax.random.fold_in(keys[6], part), 7)
    return {
        "tiles": gaussian(part_keys[0], (N_AUX * SLOTS, TILE, TILE), (N_AUX * SLOTS * TILE * TILE // (2 * NAUX)) ** -0.5, 0.25, ((0, 4),)),
        "slot_aux": draw_slot_aux(jax.random.fold_in(jax.random.fold_in(keys[6], part), 71), part),
        "slot_basis": draw_slot_basis(jax.random.fold_in(jax.random.fold_in(keys[6], part), 71), part),
        "slot_count": draw_slot_count(jax.random.fold_in(jax.random.fold_in(keys[6], part), 71), part),
        "orbitals": draw_orbitals(jax.random.fold_in(jax.random.fold_in(keys[6], part), 71), part),
        "fit_rows": draw_fit_rows(jax.random.fold_in(jax.random.fold_in(keys[6], part), 71), part),
    }


def reference(tiles, slot_aux, slot_basis, slot_count, orbitals, fit_rows):
    aux_blocks = NAUX // TILE
    panels = orbitals.astype(jnp.float32).reshape(NBAS // TILE, TILE, NOCC)
    tile_sets = tiles.reshape(N_AUX, SLOTS, TILE, TILE)
    block_slots = min(32, SLOTS)

    def one_device(running, device):
        row_count = slot_count[device]
        chosen_all = tile_sets[device]
        owners_all = slot_aux[device]
        bases_all = slot_basis[device]

        def one_block(counter, inner):
            first_slot = counter * block_slots
            begin_slot = jnp.minimum(first_slot, SLOTS - block_slots).astype(jnp.int32)
            places = begin_slot + jnp.arange(block_slots, dtype=jnp.int32)
            active = (places >= first_slot) & (places < row_count)
            chosen = lax.dynamic_slice_in_dim(chosen_all, begin_slot, block_slots, 0).astype(jnp.float32)
            bases = lax.dynamic_slice_in_dim(bases_all, begin_slot, block_slots, 0)
            owners = lax.dynamic_slice_in_dim(owners_all, begin_slot, block_slots, 0)
            halfway = jnp.einsum("spm,smo->spo", chosen, panels[bases])
            weights = jnp.where(active, 1.0, 0.0).astype(jnp.float32)
            return inner.at[owners].add(halfway * weights[:, None, None])

        steps_needed = ((row_count + block_slots - 1) // block_slots).astype(jnp.int32)
        return lax.fori_loop(jnp.int32(0), steps_needed, one_block, running), None

    coeffs, _ = lax.scan(one_device, jnp.zeros((aux_blocks, TILE, NOCC), jnp.float32), jnp.arange(N_AUX, dtype=jnp.int32))
    rounded = coeffs.reshape(NAUX, NOCC).astype(jnp.bfloat16)
    fitted = jnp.dot(fit_rows, rounded, preferred_element_type=jnp.float32).astype(jnp.bfloat16)
    return jnp.dot(fitted.T, fitted, preferred_element_type=jnp.float32)
```

```python
import functools

import jax
import jax.numpy as jnp
from jax import lax
from jax.experimental import pallas as pl
from jax.experimental.pallas import tpu as pltpu
from jax.sharding import PartitionSpec as P

LANES = 128
CHUNKS = 16
LAG = 2


def rotation(size, by):
    return [(i, (i + by) % size) for i in range(size)]


def flipped(size, bit):
    return [(i, i ^ bit) for i in range(size)]


def spread_kernel(carry, sections, *refs):
    limits = refs[0]
    orbitals = refs[1 + 3 * len(sections)]
    sums = refs[-1]
    tile = orbitals.shape[0] and refs[3].shape[-1]
    groups = sums.shape[0]
    if carry:
        sums[...] = refs[-2][...]
    else:
        sums[...] = jnp.zeros_like(sums)
    at = 0
    for which, parts in enumerate(sections):
        owners, bases, tiles = refs[1 + 3 * which : 4 + 3 * which]

        def one(i, _, owners=owners, bases=bases, tiles=tiles):
            place = pl.multiple_of(owners[i] * tile, tile)
            panel = orbitals[pl.ds(pl.multiple_of(bases[i] * tile, tile), tile), :]
            term = jnp.dot(tiles[i], panel, preferred_element_type=jnp.float32)
            for g in range(groups):
                sums[g, pl.ds(place, tile), :] += term[:, g * LANES : (g + 1) * LANES]
            return 0

        for _ in range(parts):
            lax.fori_loop(limits[at], limits[at + 1], one, 0)
            at += 2


def spread(limits, sections, orbitals, rows, carried=None):
    width = orbitals.shape[1]
    groups = width // LANES
    vmem = pl.BlockSpec(memory_space=pltpu.VMEM)
    smem = pl.BlockSpec(memory_space=pltpu.SMEM)
    operands, specs, counts = [limits], [smem], []
    for owners, bases, tiles, parts in sections:
        operands += [owners, bases, tiles]
        specs += [smem, smem, vmem]
        counts.append(parts)
    operands.append(orbitals)
    specs.append(vmem)
    if carried is not None:
        operands.append(carried)
        specs.append(vmem)
    return pl.pallas_call(
        functools.partial(spread_kernel, carried is not None, tuple(counts)),
        out_shape=jax.ShapeDtypeStruct((groups, rows, LANES), jnp.float32),
        in_specs=specs,
        out_specs=vmem,
        compiler_params=pltpu.CompilerParams(vmem_limit_bytes=56 * 1024 * 1024),
        cost_estimate=pl.CostEstimate(
            flops=2 * 64 * 128 * 128 * width,
            bytes_accessed=24 * 1024 * 1024,
            transcendentals=0,
        ),
    )(*operands)


def all_planes(partial, planes, position):
    half = planes // 2
    total = partial.shape[0]
    size = total // CHUNKS
    rightward = [(i, i + 1) for i in range(planes - 1)]
    leftward = [(i + 1, i) for i in range(planes - 1)]
    mirrored = planes - 1 - position
    in_left = position < half
    hops = planes - 1
    steps = CHUNKS + LAG * hops
    gathered = jnp.zeros((total + LAG * (half - 1) * size, LANES), jnp.bfloat16)
    far = LAG * jnp.maximum(position, mirrored)
    got_right, got_left, paid_right, paid_left = {}, {}, {}, {}

    def own_rows(chunk):
        return lax.dynamic_slice_in_dim(partial, jnp.clip(chunk, 0, CHUNKS - 1) * size, size, 0)

    finished = []
    for s in range(steps):
        def payload(rank, on_my_half, got, paid_other):
            rows = own_rows(s - LAG * rank)
            before = got.get(s - LAG)
            if before is None:
                return rows.astype(jnp.bfloat16)
            crossing = paid_other[s - LAG]
            added = jnp.where(on_my_half, rows, jnp.where(rank == half, crossing.astype(jnp.float32), 0.0))
            return (before.astype(jnp.float32) + added).astype(jnp.bfloat16)

        right = payload(position, in_left, got_right, paid_left)
        left = payload(mirrored, ~in_left, got_left, paid_right)
        paid_right[s], paid_left[s] = right, left
        pairs_right = [(i, j) for i, j in rightward if 0 <= s - LAG * i < CHUNKS]
        pairs_left = [(i, j) for i, j in leftward if 0 <= s - LAG * (planes - 1 - i) < CHUNKS]
        if pairs_right:
            got_right[s] = lax.ppermute(right, "aux", pairs_right)
            got_left[s] = lax.ppermute(left, "aux", pairs_left)
        if s >= LAG * half:
            done = jnp.where(in_left, left, right)
            gathered = lax.dynamic_update_slice_in_dim(
                gathered, done, jnp.maximum(s - far, 0) * size, 0
            )
        finished.append(gathered)
    return finished, LAG * hops


def shards(tiles, slot_aux, slot_basis, slot_count, orbitals, fit_rows, *, groups, planes, across):
    position = lax.axis_index("aux")
    member = lax.axis_index("orb")
    slots, tile = tiles.shape[:2]
    aux_rows = fit_rows.shape[1]
    width = orbitals.shape[1]
    local_bases = orbitals.shape[0] // tile
    cap = min(slots, 2 * -(-7 * slots // (8 * planes)))
    part = cap // 2

    live = jnp.arange(slots, dtype=jnp.int32)[None, :] < slot_count[:, None]
    target = jnp.where(live, slot_basis // local_bases, planes)
    plane_ids = jnp.arange(planes, dtype=jnp.int32)
    begins = jnp.sum(target[:, None, :] < plane_ids[None, :, None], axis=2, dtype=jnp.int32)
    counts = jnp.sum(target[:, None, :] == plane_ids[None, :, None], axis=2, dtype=jnp.int32)
    away = jnp.where(plane_ids[:, None] == plane_ids[None, :], 0, counts)
    rounds = (jnp.max(away) + cap - 1) // cap
    most = rounds
    for by in range(1, groups):
        most = jnp.maximum(most, lax.ppermute(rounds, "groups", rotation(groups, by)))

    core = member % 2
    twins = flipped(across, 1)
    send_first = lax.dynamic_index_in_dim(begins, position, 0, keepdims=False)
    sources = (position - jnp.arange(1, planes, dtype=jnp.int32)) % planes
    get_first = lax.dynamic_index_in_dim(begins, position, 1, keepdims=False)[sources]
    get_count = lax.dynamic_index_in_dim(counts, position, 1, keepdims=False)[sources]

    def exchange(turn):
        mine = []
        for by in range(1, planes):
            first = send_first[(position + by) % planes] + turn * cap
            begin = jnp.minimum(first, slots - cap) + core * part
            chosen = lax.dynamic_slice_in_dim(tiles, begin, part, 0)
            mine.append(lax.ppermute(chosen, "aux", rotation(planes, by)))
        mine = jnp.concatenate(mine, axis=0)
        theirs = lax.ppermute(mine, "orb", twins)
        sections, limits = [], []
        first = get_first + turn * cap
        last = jnp.minimum(first + cap, get_first + get_count)
        for side, held in ((core, mine), (1 - core, theirs)):
            begin = jnp.minimum(first, slots - cap) + side * part
            offset = jnp.arange(planes - 1, dtype=jnp.int32) * part
            low = jnp.clip(first - begin, 0, part) + offset
            high = jnp.clip(last - begin, 0, part) + offset
            limits.append(jnp.stack([low, high], axis=1).reshape(-1))
            places = begin[:, None] + jnp.arange(part, dtype=jnp.int32)[None, :]
            owners = slot_aux[sources[:, None], places].reshape(-1)
            bases = slot_basis[sources[:, None], places].reshape(-1) - position * local_bases
            sections.append((owners, bases, held, planes - 1))
        return limits, sections

    limits, sections = exchange(jnp.int32(0))
    own_owners = lax.dynamic_index_in_dim(slot_aux, position, 0, keepdims=False)
    own_bases = lax.dynamic_index_in_dim(slot_basis, position, 0, keepdims=False) - position * local_bases
    own_first = send_first[position]
    own_last = own_first + counts[position, position]
    partial = spread(
        jnp.concatenate([jnp.stack([own_first, own_last])] + limits),
        [(own_owners, own_bases, tiles, 1)] + sections,
        orbitals,
        aux_rows,
    )

    def more(state):
        turn, sums = state
        limits, sections = exchange(turn)
        return turn + 1, spread(jnp.concatenate(limits), sections, orbitals, aux_rows, sums)

    _, partial = lax.while_loop(lambda state: state[0] < most, more, (jnp.int32(1), partial))

    finished, delay = all_planes(partial.reshape(-1, LANES), planes, position)
    column_groups = width // LANES
    square = planes == across == 4
    per_group = CHUNKS // column_groups
    fitted, pieces = [], []
    for g in range(column_groups):
        rounded = finished[(g + 1) * per_group - 1 + delay]
        rounded = lax.slice_in_dim(rounded, g * aux_rows, (g + 1) * aux_rows, axis=0)
        own = jnp.dot(fit_rows, rounded, preferred_element_type=jnp.float32).astype(jnp.bfloat16)
        fitted.append(own)
        if square:
            twin = lax.ppermute(own, "orb", flipped(across, 1))
            other = lax.ppermute(own, "orb", flipped(across, 2))
            last = lax.ppermute(other, "orb", flipped(across, 1))
            pieces.append(jnp.stack([own, twin, other, last]))
    fitted = jnp.concatenate(fitted, axis=1)
    if not square:
        wide = lax.all_gather(fitted, "orb", axis=1, tiled=True)
        partial = jnp.einsum("pj,pi->ji", wide, fitted, preferred_element_type=jnp.float32)
        return lax.psum_scatter(partial, "aux", scatter_dimension=0, tiled=True)
    pieces = jnp.concatenate(pieces, axis=2)
    blocks = jnp.einsum("dpj,pi->dji", pieces, fitted, preferred_element_type=jnp.float32)

    def block_for(plane):
        return lax.dynamic_index_in_dim(blocks, plane ^ member, 0, keepdims=False)

    result = block_for(position)
    for by in range(1, planes):
        away_block = block_for((position + by) % planes).astype(jnp.bfloat16)
        result += lax.ppermute(away_block, "aux", rotation(planes, by)).astype(jnp.float32)
    return result


def solution(mesh):
    body = functools.partial(
        shards,
        groups=mesh.shape["groups"],
        planes=mesh.shape["aux"],
        across=mesh.shape["orb"],
    )
    return jax.shard_map(
        body,
        mesh=mesh,
        in_specs=(
            P(("groups", "aux"), None, None),
            P("groups", None),
            P("groups", None),
            P("groups"),
            P(("groups", "aux"), "orb"),
            P(("groups", "aux"), None),
        ),
        out_specs=P(("groups", "aux"), "orb"),
        check_vma=False,
    )
```

```python
import functools

import jax
import jax.numpy as jnp
from jax import lax
from jax.experimental import pallas as pl
from jax.experimental.pallas import tpu as pltpu
from jax.sharding import PartitionSpec as P

LANES = 128
CHUNKS = 16
LAG = 2
UNROLL = 2


def rotation(size, by):
    return [(i, (i + by) % size) for i in range(size)]


def flipped(size, bit):
    return [(i, i ^ bit) for i in range(size)]


def over_members(array, axis, size):
    held = {0: array}
    bit = size // 2
    while bit:
        held |= {e | bit: lax.ppermute(a, axis, flipped(size, bit)) for e, a in held.items()}
        bit //= 2
    return [held[e] for e in range(size)]


def spread_kernel(planes, across, cap, place, table_aux, table_basis, begins, counts, own_tiles, *refs):
    received = refs[:-8]
    overflow, panels, sums, held, chosen, owners, bases, arrived = refs[-8:]
    slots, tile = own_tiles.shape[:2]
    part = cap // across
    batch = part * (planes - 1)
    position, member, rounds = place[0], place[1], place[2]
    local_bases = panels.shape[0] // tile
    groups = sums.shape[0]

    copies, at = [], 0
    for n, tiles in enumerate(received):
        copies.append(pltpu.make_async_copy(tiles, held.at[pl.ds(at, tiles.shape[0])], arrived.at[n]))
        at += tiles.shape[0]
    for copy in copies:
        copy.start()
    sums[...] = jnp.zeros_like(sums)

    def rows_of(source, slot):
        return table_aux[source, slot] * tile, (table_basis[source, slot] - position * local_bases) * tile

    def ranges(turn, side, source):
        first = begins[source, position] + turn * cap
        last = jnp.minimum(first + cap, begins[source, position] + counts[source, position])
        begin = jnp.minimum(first, slots - cap) + side * part
        return begin, jnp.clip(first - begin, 0, part), jnp.clip(last - begin, 0, part)

    def term_of(block, base):
        panel = panels[pl.ds(pl.multiple_of(base, tile), tile), :]
        return jnp.dot(block, panel, preferred_element_type=jnp.float32)

    def add(owner, term):
        for g in range(groups):
            sums[g, pl.ds(pl.multiple_of(owner, tile), tile), :] += term[:, g * LANES : (g + 1) * LANES]

    count = jnp.int32(0)
    for e in range(across):
        for q in range(planes - 1):
            source = lax.rem(position + (planes - 1 - q), planes)
            begin, low, high = ranges(0, member ^ e, source)

            def note(i, count, e=e, q=q, source=source, begin=begin):
                chosen[count] = e * batch + q * part + i
                owners[count], bases[count] = rows_of(source, begin + i)
                return count + 1

            count = lax.fori_loop(low, high, note, count)
    for i in range(UNROLL - 1):
        chosen[count + i] = 0
        owners[count + i] = 0
        bases[count + i] = 0

    own_first = begins[position, position]
    own_count = counts[position, position]

    def several_own(n, _):
        terms = []
        for i in range(UNROLL):
            used = n * UNROLL + i < own_count
            slot = jnp.minimum(own_first + n * UNROLL + i, slots - 1)
            owner, base = rows_of(position, slot)
            term = term_of(own_tiles[slot], jnp.where(used, base, 0))
            terms.append((owner, jnp.where(used, term, 0.0)))
        for owner, term in terms:
            add(owner, term)
        return 0

    lax.fori_loop(0, (own_count + UNROLL - 1) // UNROLL, several_own, 0)
    for copy in copies:
        copy.wait()

    def several(n, _):
        terms = []
        for i in range(UNROLL):
            at = n * UNROLL + i
            term = term_of(held[chosen[at]], bases[at])
            terms.append((owners[at], jnp.where(at < count, term, 0.0)))
        for owner, term in terms:
            add(owner, term)
        return 0

    lax.fori_loop(0, (count + UNROLL - 1) // UNROLL, several, 0)

    def late_round(turn, _):
        def late_part(n, _):
            e, q = n // (planes - 1), lax.rem(n, planes - 1)
            source = lax.rem(position + (planes - 1 - q), planes)
            begin, low, high = ranges(turn, member ^ e, source)

            def late_one(i, _):
                pltpu.sync_copy(overflow.at[turn - 1, e, q * part + i], held.at[0])
                owner, base = rows_of(source, begin + i)
                add(owner, term_of(held[0], base))
                return 0

            return lax.fori_loop(low, high, late_one, 0)

        return lax.fori_loop(0, across * (planes - 1), late_part, 0)

    lax.fori_loop(1, rounds, late_round, 0)


def spread(place, tables, tiles, received, overflow, orbitals, rows, planes, across, cap):
    slots, tile = tiles.shape[:2]
    most = sum(r.shape[0] for r in received)
    smem = pl.BlockSpec(memory_space=pltpu.SMEM)
    vmem = pl.BlockSpec(memory_space=pltpu.VMEM)
    hbm = pl.BlockSpec(memory_space=pltpu.HBM)
    return pl.pallas_call(
        functools.partial(spread_kernel, planes, across, cap),
        out_shape=jax.ShapeDtypeStruct((orbitals.shape[1] // LANES, rows, LANES), jnp.float32),
        in_specs=[smem] * 5 + [vmem] * (1 + len(received)) + [hbm, vmem],
        out_specs=vmem,
        scratch_shapes=[
            pltpu.VMEM((most, tile, tile), tiles.dtype),
            pltpu.SMEM((most + UNROLL,), jnp.int32),
            pltpu.SMEM((most + UNROLL,), jnp.int32),
            pltpu.SMEM((most + UNROLL,), jnp.int32),
            pltpu.SemaphoreType.DMA((len(received),)),
        ],
        compiler_params=pltpu.CompilerParams(vmem_limit_bytes=24 * 1024 * 1024),
        cost_estimate=pl.CostEstimate(
            flops=2 * slots * tile * tile * orbitals.shape[1],
            bytes_accessed=24 * 1024 * 1024,
            transcendentals=0,
        ),
    )(place, *tables, tiles, *received, overflow, orbitals)


def stage_kernel(steps, tiles, source, staged, largest, arrived):
    size = source.shape[0] // steps

    def piece(n):
        rows = pl.ds(n * size, size)
        return pltpu.make_async_copy(source.at[rows], staged.at[rows], arrived.at[n])

    for n in range(steps):
        piece(n).start()
    lanes = tiles.shape[-1]
    best = jnp.max(jnp.abs(tiles[...].reshape(-1, 16, lanes)), axis=0)
    largest[0] = best.astype(jnp.float32)
    most = None
    for n in range(steps):
        piece(n).wait()
        block = jnp.abs(staged[pl.ds(n * size, size), :]).reshape(-1, 16, source.shape[1])
        found = jnp.max(block, axis=0)
        most = found if most is None else jnp.maximum(most, found)
    across = most[:, :lanes]
    for g in range(1, source.shape[1] // lanes):
        across = jnp.maximum(across, most[:, g * lanes : (g + 1) * lanes])
    largest[1] = across.astype(jnp.float32)


def stage(tiles, orbitals):
    steps = 8
    vmem = pl.BlockSpec(memory_space=pltpu.VMEM)
    return pl.pallas_call(
        functools.partial(stage_kernel, steps),
        out_shape=(
            jax.ShapeDtypeStruct(orbitals.shape, orbitals.dtype),
            jax.ShapeDtypeStruct((2, 16, tiles.shape[-1]), jnp.float32),
        ),
        in_specs=[vmem, pl.BlockSpec(memory_space=pltpu.HBM)],
        out_specs=(vmem, vmem),
        scratch_shapes=[pltpu.SemaphoreType.DMA((steps,))],
        compiler_params=pltpu.CompilerParams(vmem_limit_bytes=16 * 1024 * 1024),
        cost_estimate=pl.CostEstimate(flops=0, bytes_accessed=10 * 1024 * 1024, transcendentals=0),
    )(tiles, orbitals)


def unfilled(shape, dtype):
    return pl.pallas_call(
        lambda out: None,
        out_shape=jax.ShapeDtypeStruct(shape, dtype),
        out_specs=pl.BlockSpec(memory_space=pltpu.HBM),
    )()


def all_planes(partial, consume, at_step, groups, rows, planes, position, scale):
    half = planes // 2
    per_group = CHUNKS // groups
    size = rows // per_group
    hops = planes - 1
    mirrored = hops - position
    in_left = position < half
    far = jnp.maximum(position, mirrored)
    got_right, got_left, paid_right, paid_left, done = {}, {}, {}, {}, {}
    total_steps = CHUNKS + LAG * hops

    def own_rows(s, rank):
        chunks = [s - LAG * r for r in range(half)]
        if not any(0 <= c < CHUNKS for c in chunks):
            return None
        at = jnp.clip(s - LAG * rank, 0, CHUNKS - 1) * size
        return lax.dynamic_slice_in_dim(partial, at, size, 0)

    def payload(s, rank, got, paid_other):
        rows = own_rows(s, rank)
        total = None if rows is None else rows * scale
        before = got.get(s - LAG)
        if before is not None:
            crossing = jnp.where(rank == half, paid_other[s - LAG].astype(jnp.float32), 0.0)
            added = crossing if total is None else jnp.where(rank < half, total, crossing)
            total = before.astype(jnp.float32) + added
        return total.astype(jnp.float16)

    def finished(group):
        pieces = []
        for k in range(group * per_group, (group + 1) * per_group):
            chunk = None
            for r in range(half, planes):
                this = done[k + LAG * r]
                chunk = this if chunk is None else jnp.where(far == r, this, chunk)
            pieces.append(chunk)
        whole = jnp.concatenate(pieces, axis=0).astype(jnp.float32)
        return lax.optimization_barrier((whole * (1.0 / scale)).astype(jnp.bfloat16))

    waiting = []
    for s in range(total_steps):
        if s - LAG in got_right:
            got_right[s - LAG], got_left[s - LAG], *_ = lax.optimization_barrier(
                (got_right[s - LAG], got_left[s - LAG], paid_right[s - 1], paid_left[s - 1], *waiting)
            )
            waiting = []
        paid_right[s] = payload(s, position, got_right, paid_left)
        paid_left[s] = payload(s, mirrored, got_left, paid_right)
        right = [(i, i + 1) for i in range(hops) if 0 <= s - LAG * i < CHUNKS]
        if right:
            got_right[s] = lax.ppermute(paid_right[s], "aux", right)
            got_left[s] = lax.ppermute(paid_left[s], "aux", [(hops - i, hops - j) for i, j in right])
        done[s] = jnp.where(in_left, paid_left[s], paid_right[s])
        group, rest = divmod(s - LAG * hops + 1, per_group)
        if group > 0 and rest == 0:
            waiting.append(consume(group - 1, finished(group - 1)))
        waiting += at_step(total_steps - s)


def shards(tiles, slot_aux, slot_basis, slot_count, orbitals, fit_rows, *, groups, planes, across):
    position = lax.axis_index("aux")
    member = lax.axis_index("orb")
    slots, tile = tiles.shape[:2]
    aux_rows = fit_rows.shape[1]
    width = orbitals.shape[1]
    local_bases = orbitals.shape[0] // tile
    cap = min(slots, across * -(-7 * slots // (4 * planes * across)))
    part = cap // across
    later = -(-slots // cap) - 1

    live = jnp.arange(slots, dtype=jnp.int32)[None, :] < slot_count[:, None]
    target = jnp.where(live, slot_basis // local_bases, planes)
    plane_ids = jnp.arange(planes, dtype=jnp.int32)
    begins = jnp.sum(target[:, None, :] < plane_ids[None, :, None], axis=2, dtype=jnp.int32)
    counts = jnp.sum(target[:, None, :] == plane_ids[None, :, None], axis=2, dtype=jnp.int32)
    away = jnp.where(plane_ids[:, None] == plane_ids[None, :], 0, counts)
    rounds = (jnp.max(away) + cap - 1) // cap
    send_first = lax.dynamic_index_in_dim(begins, position, 0, keepdims=False)

    def exchange(turn):
        chosen = []
        for by in range(1, planes):
            first = send_first[(position + by) % planes] + turn * cap
            begin = jnp.minimum(first, slots - cap) + member * part
            chosen.append(lax.dynamic_slice_in_dim(tiles, begin, part, 0))
        chosen = lax.optimization_barrier(chosen)
        sent = [lax.ppermute(c, "aux", rotation(planes, by)) for by, c in enumerate(chosen, 1)]
        return chosen, sent

    def gather(sent):
        if planes > 4:
            sent = [jnp.concatenate(sent, axis=0)]
        held = [over_members(arrived, "orb", across) for arrived in sent]
        return [[h[e] for h in held] for e in range(across)]

    chosen, sent = exchange(jnp.int32(0))
    all_tiles, all_orbitals, _ = lax.optimization_barrier((tiles, orbitals, chosen))
    panels, largest = stage(all_tiles, all_orbitals)
    largest = jnp.max(largest, axis=(1, 2))
    *sent, largest, rounds = lax.optimization_barrier((*sent, largest, rounds))
    largest = jnp.broadcast_to(largest[:, None], (2, LANES))
    others = [lax.ppermute(largest, "aux", rotation(planes, by)) for by in range(1, planes)]
    most = rounds
    for by in range(1, groups):
        most = jnp.maximum(most, lax.ppermute(rounds, "groups", rotation(groups, by)))
    received = [part_tiles for entry in gather(sent) for part_tiles in entry]
    for other in others:
        largest = jnp.maximum(largest, other)
    bound = tile * jnp.sum(counts).astype(jnp.float32) * largest[0, 0] * largest[1, 0]
    scale = 32768.0 / jnp.maximum(bound, 1e-30)

    def more(state):
        turn, kept = state
        tiles_now = jnp.stack([jnp.concatenate(entry, axis=0) for entry in gather(exchange(turn)[1])])
        return turn + 1, lax.dynamic_update_index_in_dim(kept, tiles_now, turn - 1, 0)

    batch = (planes - 1) * part
    empty = unfilled((max(later, 1), across, batch, tile, tile), tiles.dtype)
    _, overflow = lax.while_loop(lambda state: state[0] < most, more, (jnp.int32(1), empty))
    place = jnp.stack([position, member, most]).astype(jnp.int32)

    tables = (slot_aux, slot_basis, begins, counts)
    partial = spread(place, tables, tiles, received, overflow, panels, aux_rows, planes, across, cap)
    partial = partial.reshape(-1, LANES)
    column_groups = width // LANES
    fitted, wide = [], []
    square = planes == across
    blocks = {}

    def product(left, right):
        return jnp.einsum("pj,pi->ji", left, right, preferred_element_type=jnp.float32)

    def scatter(parts):
        stacked = jnp.stack(parts)

        def to(plane):
            return lax.dynamic_index_in_dim(stacked, plane ^ member, 0, keepdims=False)

        sent = [to((position + by) % planes).astype(jnp.bfloat16) for by in range(1, planes)]
        return [to(position)] + [lax.ppermute(t, "aux", rotation(planes, by)) for by, t in enumerate(sent, 1)]

    def total(terms):
        return sum((t.astype(jnp.float32) for t in terms[1:]), terms[0])

    def consume(g, rounded):
        last = g == column_groups - 1
        if square and last:
            rounded, blocks["corner"][1] = lax.optimization_barrier((rounded, blocks["corner"][1]))
        own = jnp.dot(fit_rows, rounded, preferred_element_type=jnp.float32).astype(jnp.bfloat16)
        if square and last:
            blocks["upper"] = scatter([product(w, own) for w in blocks["early"]])
        fitted.append(own)
        if square:
            wide.append(over_members(own, "orb", across))
        if square and g == column_groups - 2:
            blocks["early"] = [jnp.concatenate([w[e] for w in wide], axis=1) for e in range(across)]
            inner = jnp.concatenate(fitted, axis=1)
            blocks["terms"] = [product(w, inner) for w in blocks["early"]]
        return own

    def at_step(steps_left):
        if "terms" in blocks and "corner" not in blocks and steps_left <= 3:
            blocks["corner"] = scatter(blocks["terms"])
            return list(blocks["terms"])
        return []

    all_planes(partial, consume, at_step, column_groups, aux_rows, planes, position, scale)
    fitted = jnp.concatenate(fitted, axis=1)
    if square:
        lower = total(scatter([product(w, fitted) for w in wide[-1]]))
        upper = jnp.concatenate([total(blocks["corner"]), total(blocks["upper"])], axis=1)
        return jnp.concatenate([upper, lower], axis=0)
    wide = lax.all_gather(fitted, "orb", axis=1, tiled=True)
    return lax.psum_scatter(product(wide, fitted), "aux", scatter_dimension=0, tiled=True)


def solution(mesh):
    body = functools.partial(
        shards,
        groups=mesh.shape["groups"],
        planes=mesh.shape["aux"],
        across=mesh.shape["orb"],
    )
    return jax.shard_map(
        body,
        mesh=mesh,
        in_specs=(
            P(("groups", "aux"), None, None),
            P("groups", None),
            P("groups", None),
            P("groups"),
            P(("groups", "aux"), "orb"),
            P(("groups", "aux"), None),
        ),
        out_specs=P(("groups", "aux"), "orb"),
        check_vma=False,
    )
```

```python
import functools

import jax
import jax.numpy as jnp
from jax import lax
from jax.experimental import pallas as pl
from jax.experimental.pallas import tpu as pltpu
from jax.sharding import PartitionSpec as P

LANES = 128
CHUNKS = 16
LAG = 2
UNROLL = 2


def rotation(size, by):
    return [(i, (i + by) % size) for i in range(size)]


def flipped(size, bit):
    return [(i, i ^ bit) for i in range(size)]


def over_members(array, axis, size, first=None):
    held = {0: array} | (first or {})
    bit = size // 4 if first else size // 2
    while bit:
        held |= {e | bit: lax.ppermute(a, axis, flipped(size, bit)) for e, a in held.items()}
        bit //= 2
    return [held[e] for e in range(size)]


def spread_kernel(planes, across, cap, place, table_aux, table_basis, begins, counts, own_tiles, *refs):
    received = refs[:-10]
    overflow, orbitals, sums, own, panels, held, chosen, owners, bases, arrived = refs[-10:]
    slots, tile = own_tiles.shape[:2]
    part = cap // across
    batch = part * (planes - 1)
    position, member, rounds = place[0], place[1], place[2]
    local_bases = panels.shape[0] // tile
    groups = sums.shape[0]

    early = [
        pltpu.make_async_copy(own_tiles, own, arrived.at[len(received)]),
        pltpu.make_async_copy(orbitals, panels, arrived.at[len(received) + 1]),
    ]
    for copy in early:
        copy.start()
    copies, at = [], 0
    for n, tiles in enumerate(received):
        copies.append(pltpu.make_async_copy(tiles, held.at[pl.ds(at, tiles.shape[0])], arrived.at[n]))
        at += tiles.shape[0]
    for copy in copies:
        copy.start()
    sums[...] = jnp.zeros_like(sums)

    def rows_of(source, slot):
        return table_aux[source, slot] * tile, (table_basis[source, slot] - position * local_bases) * tile

    def ranges(turn, side, source):
        first = begins[source, position] + turn * cap
        last = jnp.minimum(first + cap, begins[source, position] + counts[source, position])
        begin = jnp.minimum(first, slots - cap) + side * part
        return begin, jnp.clip(first - begin, 0, part), jnp.clip(last - begin, 0, part)

    def term_of(block, base):
        panel = panels[pl.ds(pl.multiple_of(base, tile), tile), :]
        return jnp.dot(block, panel, preferred_element_type=jnp.float32)

    def add(owner, term):
        for g in range(groups):
            sums[g, pl.ds(pl.multiple_of(owner, tile), tile), :] += term[:, g * LANES : (g + 1) * LANES]

    count = jnp.int32(0)
    for e in range(across):
        for q in range(planes - 1):
            source = lax.rem(position + (planes - 1 - q), planes)
            begin, low, high = ranges(0, member ^ e, source)

            def note(i, count, e=e, q=q, source=source, begin=begin):
                chosen[count] = e * batch + q * part + i
                owners[count], bases[count] = rows_of(source, begin + i)
                return count + 1

            count = lax.fori_loop(low, high, note, count)
    for i in range(UNROLL - 1):
        chosen[count + i] = 0
        owners[count + i] = 0
        bases[count + i] = 0

    for copy in early:
        copy.wait()
    own_first = begins[position, position]
    own_count = counts[position, position]

    def several_own(n, _):
        terms = []
        for i in range(UNROLL):
            used = n * UNROLL + i < own_count
            slot = jnp.minimum(own_first + n * UNROLL + i, slots - 1)
            owner, base = rows_of(position, slot)
            term = term_of(own[slot], jnp.where(used, base, 0))
            terms.append((owner, jnp.where(used, term, 0.0)))
        for owner, term in terms:
            add(owner, term)
        return 0

    lax.fori_loop(0, (own_count + UNROLL - 1) // UNROLL, several_own, 0)
    for copy in copies:
        copy.wait()

    def several(n, _):
        terms = []
        for i in range(UNROLL):
            at = n * UNROLL + i
            term = term_of(held[chosen[at]], bases[at])
            terms.append((owners[at], jnp.where(at < count, term, 0.0)))
        for owner, term in terms:
            add(owner, term)
        return 0

    lax.fori_loop(0, (count + UNROLL - 1) // UNROLL, several, 0)

    def late_round(turn, _):
        def late_part(n, _):
            e, q = n // (planes - 1), lax.rem(n, planes - 1)
            source = lax.rem(position + (planes - 1 - q), planes)
            begin, low, high = ranges(turn, member ^ e, source)

            def late_one(i, _):
                pltpu.sync_copy(overflow.at[turn - 1, e, q * part + i], held.at[0])
                owner, base = rows_of(source, begin + i)
                add(owner, term_of(held[0], base))
                return 0

            return lax.fori_loop(low, high, late_one, 0)

        return lax.fori_loop(0, across * (planes - 1), late_part, 0)

    lax.fori_loop(1, rounds, late_round, 0)


def spread(place, tables, tiles, received, overflow, orbitals, rows, planes, across, cap):
    slots, tile = tiles.shape[:2]
    most = sum(r.shape[0] for r in received)
    smem = pl.BlockSpec(memory_space=pltpu.SMEM)
    vmem = pl.BlockSpec(memory_space=pltpu.VMEM)
    hbm = pl.BlockSpec(memory_space=pltpu.HBM)
    return pl.pallas_call(
        functools.partial(spread_kernel, planes, across, cap),
        out_shape=jax.ShapeDtypeStruct((orbitals.shape[1] // LANES, rows, LANES), jnp.float32),
        in_specs=[smem] * 5 + [hbm] * (1 + len(received) + 2),
        out_specs=vmem,
        scratch_shapes=[
            pltpu.VMEM(tiles.shape, tiles.dtype),
            pltpu.VMEM(orbitals.shape, orbitals.dtype),
            pltpu.VMEM((most, tile, tile), tiles.dtype),
            pltpu.SMEM((most + UNROLL,), jnp.int32),
            pltpu.SMEM((most + UNROLL,), jnp.int32),
            pltpu.SMEM((most + UNROLL,), jnp.int32),
            pltpu.SemaphoreType.DMA((len(received) + 2,)),
        ],
        compiler_params=pltpu.CompilerParams(vmem_limit_bytes=52 * 1024 * 1024),
        cost_estimate=pl.CostEstimate(
            flops=2 * slots * tile * tile * orbitals.shape[1],
            bytes_accessed=24 * 1024 * 1024,
            transcendentals=0,
        ),
    )(place, *tables, tiles, *received, overflow, orbitals)


def largest_kernel(steps, tiles, source, largest, panels, blocks, arrived):
    size = source.shape[0] // steps
    lanes = tiles.shape[-1]

    def piece(n):
        rows = pl.ds(n * size, size)
        return pltpu.make_async_copy(source.at[rows], panels.at[rows], arrived.at[n])

    whole = pltpu.make_async_copy(tiles, blocks, arrived.at[steps])
    whole.start()
    for n in range(steps):
        piece(n).start()
    whole.wait()
    largest[0] = jnp.max(jnp.abs(blocks[...].reshape(-1, 16, lanes)), axis=0).astype(jnp.float32)
    most = None
    for n in range(steps):
        piece(n).wait()
        block = jnp.abs(panels[pl.ds(n * size, size), :]).reshape(-1, 16, source.shape[1])
        found = jnp.max(block, axis=0)
        most = found if most is None else jnp.maximum(most, found)
    across = most[:, :lanes]
    for g in range(1, source.shape[1] // lanes):
        across = jnp.maximum(across, most[:, g * lanes : (g + 1) * lanes])
    largest[1] = across.astype(jnp.float32)


def largest_of(tiles, orbitals):
    steps = 8
    hbm = pl.BlockSpec(memory_space=pltpu.HBM)
    return pl.pallas_call(
        functools.partial(largest_kernel, steps),
        out_shape=jax.ShapeDtypeStruct((2, 16, tiles.shape[-1]), jnp.float32),
        in_specs=[hbm, hbm],
        out_specs=pl.BlockSpec(memory_space=pltpu.VMEM),
        scratch_shapes=[
            pltpu.VMEM(orbitals.shape, orbitals.dtype),
            pltpu.VMEM(tiles.shape, tiles.dtype),
            pltpu.SemaphoreType.DMA((steps + 1,)),
        ],
        compiler_params=pltpu.CompilerParams(vmem_limit_bytes=52 * 1024 * 1024),
        cost_estimate=pl.CostEstimate(flops=0, bytes_accessed=10 * 1024 * 1024, transcendentals=0),
    )(tiles, orbitals)


def unfilled(shape, dtype):
    return pl.pallas_call(
        lambda out: None,
        out_shape=jax.ShapeDtypeStruct(shape, dtype),
        out_specs=pl.BlockSpec(memory_space=pltpu.HBM),
    )()


def all_planes(partial, consume, at_step, groups, rows, planes, position, scale):
    half = planes // 2
    per_group = CHUNKS // groups
    size = rows // per_group
    hops = planes - 1
    mirrored = hops - position
    in_left = position < half
    even = position % 2 == 0
    far = jnp.maximum(position, mirrored)
    got, paid = {}, {}
    total_steps = CHUNKS + LAG * hops

    def own_rows(s, rank):
        chunks = [s - LAG * r for r in range(half)]
        if not any(0 <= c < CHUNKS for c in chunks):
            return None
        at = jnp.clip(s - LAG * rank, 0, CHUNKS - 1) * size
        return lax.dynamic_slice_in_dim(partial, at, size, 0)

    def payload(s, rank, before, crossing):
        rows = own_rows(s, rank)
        total = None if rows is None else rows * scale
        if before is not None:
            crossing = jnp.where(rank == half, crossing.astype(jnp.float32), 0.0)
            added = crossing if total is None else jnp.where(rank < half, total, crossing)
            total = before.astype(jnp.float32) + added
        return total.astype(jnp.float16)

    def payloads(s):
        right_before = left_before = right_paid = left_paid = None
        if s - LAG in got:
            over_even, over_odd = got[s - LAG]
            right_before, left_before = jnp.where(even, over_odd, over_even), jnp.where(even, over_even, over_odd)
            over_even, over_odd = paid[s - LAG]
            right_paid, left_paid = jnp.where(even, over_even, over_odd), jnp.where(even, over_odd, over_even)
        right = payload(s, position, right_before, left_paid)
        left = payload(s, mirrored, left_before, right_paid)
        return jnp.where(even, right, left), jnp.where(even, left, right)

    def finished(group):
        pieces = []
        for k in range(group * per_group, (group + 1) * per_group):
            chunk = None
            for r in range(half, planes):
                over_even, over_odd = paid[k + LAG * r]
                this = jnp.where(in_left == even, over_odd, over_even)
                chunk = this if chunk is None else jnp.where(far == r, this, chunk)
            pieces.append(chunk)
        whole = jnp.concatenate(pieces, axis=0).astype(jnp.float32)
        return lax.optimization_barrier((whole * (1.0 / scale)).astype(jnp.bfloat16))

    waiting = []
    for s in range(total_steps):
        if s - LAG in got:
            got[s - LAG], *_ = lax.optimization_barrier((got[s - LAG], paid[s - 1], *waiting))
            waiting = []
        paid[s] = payloads(s)
        links = ([], [])
        for i in range(hops):
            if 0 <= s - LAG * i < CHUNKS:
                links[i % 2].append((i, i + 1))
            if 0 <= s - LAG * (hops - 1 - i) < CHUNKS:
                links[i % 2].append((i + 1, i))
        if links[0] or links[1]:
            got[s] = tuple(
                lax.ppermute(p, "aux", pairs) if pairs else jnp.zeros_like(p) for p, pairs in zip(paid[s], links)
            )
        group, rest = divmod(s - LAG * hops + 1, per_group)
        if group > 0 and rest == 0:
            waiting.append(consume(group - 1, finished(group - 1)))
        waiting += at_step(total_steps - s)


def shards(tiles, slot_aux, slot_basis, slot_count, orbitals, fit_rows, *, groups, planes, across):
    position = lax.axis_index("aux")
    member = lax.axis_index("orb")
    slots, tile = tiles.shape[:2]
    aux_rows = fit_rows.shape[1]
    width = orbitals.shape[1]
    local_bases = orbitals.shape[0] // tile
    cap = min(slots, across * -(-7 * slots // (4 * planes * across)))
    part = cap // across
    later = -(-slots // cap) - 1

    live = jnp.arange(slots, dtype=jnp.int32)[None, :] < slot_count[:, None]
    target = jnp.where(live, slot_basis // local_bases, planes)
    plane_ids = jnp.arange(planes, dtype=jnp.int32)
    begins = jnp.sum(target[:, None, :] < plane_ids[None, :, None], axis=2, dtype=jnp.int32)
    counts = jnp.sum(target[:, None, :] == plane_ids[None, :, None], axis=2, dtype=jnp.int32)
    away = jnp.where(plane_ids[:, None] == plane_ids[None, :], 0, counts)
    rounds = (jnp.max(away) + cap - 1) // cap
    send_first = lax.dynamic_index_in_dim(begins, position, 0, keepdims=False)

    def exchange(turn):
        chosen = []
        for by in range(1, planes):
            first = send_first[(position + by) % planes] + turn * cap
            begin = jnp.minimum(first, slots - cap) + member * part
            chosen.append(lax.dynamic_slice_in_dim(tiles, begin, part, 0))
        return lax.optimization_barrier(chosen)

    def over_planes(chosen):
        return [lax.ppermute(c, "aux", rotation(planes, by)) for by, c in enumerate(chosen, 1)]

    def gather(sent):
        held = [over_members(arrived, "orb", across) for arrived in sent]
        return [[h[e] for h in held] for e in range(across)]

    def bound_of(largest):
        largest = jnp.broadcast_to(jnp.max(largest, axis=(1, 2))[:, None], (2, LANES))
        return [largest] + [lax.ppermute(largest, "aux", rotation(planes, by)) for by in range(1, planes)]

    chosen = exchange(jnp.int32(0))
    all_tiles, all_orbitals, rounds, _ = lax.optimization_barrier((tiles, orbitals, rounds, chosen))
    largest = largest_of(all_tiles, all_orbitals)
    most = rounds
    for by in range(1, groups):
        most = jnp.maximum(most, lax.ppermute(rounds, "groups", rotation(groups, by)))
    if planes == 4:
        first_hop = flipped(across, across // 2)
        sent, hopped = [lax.ppermute(chosen[0], "aux", rotation(planes, 1))], []
        later_tiles, sent[0], largest = lax.optimization_barrier((chosen[1], sent[0], largest))
        others = bound_of(largest)
        sent.append(lax.ppermute(later_tiles, "aux", rotation(planes, 2)))
        hopped.append(lax.ppermute(sent[0], "orb", first_hop))
        later_tiles, sent[1], hopped[0], others = lax.optimization_barrier((chosen[2], sent[1], hopped[0], others))
        sent.append(lax.ppermute(later_tiles, "aux", rotation(planes, 3)))
        hopped.append(lax.ppermute(sent[1], "orb", first_hop))
        sent[2], hopped[1], most = lax.optimization_barrier((sent[2], hopped[1], most))
        hopped.append(lax.ppermute(sent[2], "orb", first_hop))
        held = [over_members(a, "orb", across, {across // 2: h}) for a, h in zip(sent, hopped)]
        received = [h[e] for e in range(across) for h in held]
    else:
        others = bound_of(largest)
        received = gather([jnp.concatenate(over_planes(chosen), axis=0)])
        received = [part_tiles for entry in received for part_tiles in entry]
    largest = functools.reduce(jnp.maximum, others)
    bound = tile * jnp.sum(counts).astype(jnp.float32) * largest[0, 0] * largest[1, 0]
    scale = 32768.0 / jnp.maximum(bound, 1e-30)

    def more(state):
        turn, kept = state
        tiles_now = jnp.stack([jnp.concatenate(entry, axis=0) for entry in gather(over_planes(exchange(turn)))])
        return turn + 1, lax.dynamic_update_index_in_dim(kept, tiles_now, turn - 1, 0)

    batch = (planes - 1) * part
    empty = unfilled((max(later, 1), across, batch, tile, tile), tiles.dtype)
    _, overflow = lax.while_loop(lambda state: state[0] < most, more, (jnp.int32(1), empty))
    place = jnp.stack([position, member, most]).astype(jnp.int32)

    tables = (slot_aux, slot_basis, begins, counts)
    partial = spread(place, tables, tiles, received, overflow, orbitals, aux_rows, planes, across, cap)
    partial = partial.reshape(-1, LANES)
    column_groups = width // LANES
    fitted, wide = [], []
    square = planes == across
    blocks = {}

    def product(left, right):
        return jnp.einsum("pj,pi->ji", left, right, preferred_element_type=jnp.float32)

    def scatter(parts):
        stacked = jnp.stack(parts)

        def to(plane):
            return lax.dynamic_index_in_dim(stacked, plane ^ member, 0, keepdims=False)

        sent = [to((position + by) % planes).astype(jnp.bfloat16) for by in range(1, planes)]
        return [to(position)] + [lax.ppermute(t, "aux", rotation(planes, by)) for by, t in enumerate(sent, 1)], sent

    def total(terms):
        return sum((t.astype(jnp.float32) for t in terms[1:]), terms[0])

    def consume(g, rounded):
        last = g == column_groups - 1
        if square and last:
            rounded, _ = lax.optimization_barrier((rounded, blocks["corner_sent"]))
        own = jnp.dot(fit_rows, rounded, preferred_element_type=jnp.float32).astype(jnp.bfloat16)
        if square and last:
            blocks["upper"], _ = scatter([product(w, own) for w in blocks["early"]])
        fitted.append(own)
        if square:
            wide.append(over_members(own, "orb", across))
        if square and g == column_groups - 2:
            blocks["early"] = [jnp.concatenate([w[e] for w in wide], axis=1) for e in range(across)]
            inner = jnp.concatenate(fitted, axis=1)
            blocks["terms"] = [product(w, inner) for w in blocks["early"]]
        return own

    def at_step(steps_left):
        if "terms" in blocks and "corner" not in blocks and steps_left <= 3:
            blocks["corner"], blocks["corner_sent"] = scatter(blocks["terms"])
            return list(blocks["terms"])
        return []

    all_planes(partial, consume, at_step, column_groups, aux_rows, planes, position, scale)
    fitted = jnp.concatenate(fitted, axis=1)
    if square:
        lower = total(scatter([product(w, fitted) for w in wide[-1]])[0])
        upper = jnp.concatenate([total(blocks["corner"]), total(blocks["upper"])], axis=1)
        return jnp.concatenate([upper, lower], axis=0)
    wide = lax.all_gather(fitted, "orb", axis=1, tiled=True)
    return lax.psum_scatter(product(wide, fitted), "aux", scatter_dimension=0, tiled=True)


def solution(mesh):
    body = functools.partial(
        shards,
        groups=mesh.shape["groups"],
        planes=mesh.shape["aux"],
        across=mesh.shape["orb"],
    )
    return jax.shard_map(
        body,
        mesh=mesh,
        in_specs=(
            P(("groups", "aux"), None, None),
            P("groups", None),
            P("groups", None),
            P("groups"),
            P(("groups", "aux"), "orb"),
            P(("groups", "aux"), None),
        ),
        out_specs=P(("groups", "aux"), "orb"),
        check_vma=False,
    )
```

```python
import functools
import math

import jax
import jax.numpy as jnp
from jax import lax
from jax.experimental import pallas as pl
from jax.experimental.pallas import tpu as pltpu
from jax.sharding import PartitionSpec as P

LANES = 128
CHUNKS = 16
LAG = 2
UNROLL = 2


def rotation(size, by):
    return [(i, (i + by) % size) for i in range(size)]


def flipped(size, bit):
    return [(i, i ^ bit) for i in range(size)]


def over_members(array, axis, size, first=None):
    held = {0: array} | (first or {})
    bit = size // 4 if first else size // 2
    while bit:
        held |= {e | bit: lax.ppermute(a, axis, flipped(size, bit)) for e, a in held.items()}
        bit //= 2
    return [held[e] for e in range(size)]


def spread_kernel(planes, across, cap, place, table_aux, table_basis, begins, counts, own_tiles, *refs):
    received = refs[:-10]
    overflow, orbitals, sums, own, panels, held, chosen, owners, bases, arrived = refs[-10:]
    slots, tile = own_tiles.shape[:2]
    part = cap // across
    position, member, rounds = place[0], place[1], place[2]
    local_bases = panels.shape[0] // tile
    groups = sums.shape[0]

    early = [
        pltpu.make_async_copy(own_tiles, own, arrived.at[len(received)]),
        pltpu.make_async_copy(orbitals, panels, arrived.at[len(received) + 1]),
    ]
    for copy in early:
        copy.start()
    copies, at = [], 0
    for n, tiles in enumerate(received):
        copies.append(pltpu.make_async_copy(tiles, held.at[pl.ds(at, tiles.shape[0])], arrived.at[n]))
        at += tiles.shape[0]
    for copy in copies:
        copy.start()

    def clear(n, _):
        for g in range(groups):
            sums[g, pl.ds(pl.multiple_of(n * tile, tile), tile), :] = jnp.zeros((tile, LANES), jnp.float32)
        return 0

    lax.fori_loop(0, sums.shape[1] // tile, clear, 0)

    def rows_of(source, slot):
        return table_aux[source, slot] * tile, (table_basis[source, slot] - position * local_bases) * tile

    def ranges(turn, side, source):
        first = begins[source, position] + turn * cap
        last = jnp.minimum(first + cap, begins[source, position] + counts[source, position])
        begin = jnp.minimum(first, slots - cap) + side * part
        return begin, jnp.clip(first - begin, 0, part), jnp.clip(last - begin, 0, part)

    def term_of(block, base):
        panel = panels[pl.ds(pl.multiple_of(base, tile), tile), :]
        return jnp.dot(block, panel, preferred_element_type=jnp.float32)

    def add(owner, term):
        for g in range(groups):
            sums[g, pl.ds(pl.multiple_of(owner, tile), tile), :] += term[:, g * LANES : (g + 1) * LANES]

    def note_part(n, count):
        e, q = n // (planes - 1), lax.rem(n, planes - 1)
        source = lax.rem(position + (planes - 1 - q), planes)
        begin, low, high = ranges(0, member ^ e, source)

        def note(i, count):
            chosen[count] = n * part + i
            owners[count], bases[count] = rows_of(source, begin + i)
            return count + 1

        return lax.fori_loop(low, high, note, count)

    count = lax.fori_loop(0, across * (planes - 1), note_part, jnp.int32(0))
    for i in range(UNROLL - 1):
        chosen[count + i] = 0
        owners[count + i] = 0
        bases[count + i] = 0

    for copy in early:
        copy.wait()
    own_first = begins[position, position]
    own_count = counts[position, position]

    def several_own(n, _):
        terms = []
        for i in range(UNROLL):
            used = n * UNROLL + i < own_count
            slot = jnp.minimum(own_first + n * UNROLL + i, slots - 1)
            owner, base = rows_of(position, slot)
            term = term_of(own[slot], jnp.where(used, base, 0))
            terms.append((owner, jnp.where(used, term, 0.0)))
        for owner, term in terms:
            add(owner, term)
        return 0

    lax.fori_loop(0, (own_count + UNROLL - 1) // UNROLL, several_own, 0)
    for copy in copies:
        copy.wait()

    def several(n, _):
        terms = []
        for i in range(UNROLL):
            at = n * UNROLL + i
            term = term_of(held[chosen[at]], bases[at])
            terms.append((owners[at], jnp.where(at < count, term, 0.0)))
        for owner, term in terms:
            add(owner, term)
        return 0

    lax.fori_loop(0, (count + UNROLL - 1) // UNROLL, several, 0)

    def late_round(turn, _):
        def late_part(n, _):
            e, q = n // (planes - 1), lax.rem(n, planes - 1)
            source = lax.rem(position + (planes - 1 - q), planes)
            begin, low, high = ranges(turn, member ^ e, source)

            def late_one(i, _):
                pltpu.sync_copy(overflow.at[turn - 1, e, q * part + i], held.at[0])
                owner, base = rows_of(source, begin + i)
                add(owner, term_of(held[0], base))
                return 0

            return lax.fori_loop(low, high, late_one, 0)

        return lax.fori_loop(0, across * (planes - 1), late_part, 0)

    lax.fori_loop(1, rounds, late_round, 0)


def spread(place, tables, tiles, received, overflow, orbitals, rows, planes, across, cap):
    slots, tile = tiles.shape[:2]
    most = sum(r.shape[0] for r in received)
    smem = pl.BlockSpec(memory_space=pltpu.SMEM)
    vmem = pl.BlockSpec(memory_space=pltpu.VMEM)
    hbm = pl.BlockSpec(memory_space=pltpu.HBM)
    return pl.pallas_call(
        functools.partial(spread_kernel, planes, across, cap),
        out_shape=jax.ShapeDtypeStruct((orbitals.shape[1] // LANES, rows, LANES), jnp.float32),
        in_specs=[smem] * 5 + [hbm] * (1 + len(received) + 2),
        out_specs=vmem,
        scratch_shapes=[
            pltpu.VMEM(tiles.shape, tiles.dtype),
            pltpu.VMEM(orbitals.shape, orbitals.dtype),
            pltpu.VMEM((most, tile, tile), tiles.dtype),
            pltpu.SMEM((most + UNROLL,), jnp.int32),
            pltpu.SMEM((most + UNROLL,), jnp.int32),
            pltpu.SMEM((most + UNROLL,), jnp.int32),
            pltpu.SemaphoreType.DMA((len(received) + 2,)),
        ],
        compiler_params=pltpu.CompilerParams(vmem_limit_bytes=52 * 1024 * 1024),
        cost_estimate=pl.CostEstimate(
            flops=2 * slots * tile * tile * orbitals.shape[1],
            bytes_accessed=24 * 1024 * 1024,
            transcendentals=0,
        ),
    )(place, *tables, tiles, *received, overflow, orbitals)


def largest_kernel(steps, tiles, source, largest, panels, blocks, arrived):
    size = source.shape[0] // steps
    lanes = tiles.shape[-1]

    def piece(n):
        rows = pl.ds(n * size, size)
        return pltpu.make_async_copy(source.at[rows], panels.at[rows], arrived.at[n])

    whole = pltpu.make_async_copy(tiles, blocks, arrived.at[steps])
    whole.start()
    for n in range(steps):
        piece(n).start()
    whole.wait()

    def most_of_tile(n, most):
        return jnp.maximum(most, jnp.max(jnp.abs(blocks[n].reshape(-1, 16, lanes)), axis=0))

    most = lax.fori_loop(0, tiles.shape[0], most_of_tile, jnp.zeros((16, lanes), tiles.dtype))
    largest[0] = most.astype(jnp.float32)
    part = math.gcd(size, 240)

    def most_of_rows(n, most):
        block = panels[pl.ds(pl.multiple_of(n * part, part), part), :]
        return jnp.maximum(most, jnp.max(jnp.abs(block.reshape(-1, 16, source.shape[1])), axis=0))

    most = jnp.zeros((16, source.shape[1]), source.dtype)
    for n in range(steps):
        piece(n).wait()
        most = lax.fori_loop(n * (size // part), (n + 1) * (size // part), most_of_rows, most)
    across = most[:, :lanes]
    for g in range(1, source.shape[1] // lanes):
        across = jnp.maximum(across, most[:, g * lanes : (g + 1) * lanes])
    largest[1] = across.astype(jnp.float32)


def largest_of(tiles, orbitals):
    steps = 8
    hbm = pl.BlockSpec(memory_space=pltpu.HBM)
    return pl.pallas_call(
        functools.partial(largest_kernel, steps),
        out_shape=jax.ShapeDtypeStruct((2, 16, tiles.shape[-1]), jnp.float32),
        in_specs=[hbm, hbm],
        out_specs=pl.BlockSpec(memory_space=pltpu.VMEM),
        scratch_shapes=[
            pltpu.VMEM(orbitals.shape, orbitals.dtype),
            pltpu.VMEM(tiles.shape, tiles.dtype),
            pltpu.SemaphoreType.DMA((steps + 1,)),
        ],
        compiler_params=pltpu.CompilerParams(vmem_limit_bytes=52 * 1024 * 1024),
        cost_estimate=pl.CostEstimate(flops=0, bytes_accessed=10 * 1024 * 1024, transcendentals=0),
    )(tiles, orbitals)


def unfilled(shape, dtype):
    return pl.pallas_call(
        lambda out: None,
        out_shape=jax.ShapeDtypeStruct(shape, dtype),
        out_specs=pl.BlockSpec(memory_space=pltpu.HBM),
    )()


def all_planes(partial, consume, at_step, groups, rows, planes, position, scale):
    half = planes // 2
    per_group = CHUNKS // groups
    size = rows // per_group
    hops = planes - 1
    mirrored = hops - position
    in_left = position < half
    even = position % 2 == 0
    far = jnp.maximum(position, mirrored)
    got, paid = {}, {}
    total_steps = CHUNKS + LAG * hops

    def own_rows(s, rank):
        chunks = [s - LAG * r for r in range(half)]
        if not any(0 <= c < CHUNKS for c in chunks):
            return None
        at = jnp.clip(s - LAG * rank, 0, CHUNKS - 1) * size
        return lax.dynamic_slice_in_dim(partial, at, size, 0)

    def payload(s, rank, before, crossing):
        rows = own_rows(s, rank)
        total = None if rows is None else rows * scale
        if before is not None:
            crossing = jnp.where(rank == half, crossing.astype(jnp.float32), 0.0)
            added = crossing if total is None else jnp.where(rank < half, total, crossing)
            total = before.astype(jnp.float32) + added
        return total.astype(jnp.float16)

    def payloads(s):
        right_before = left_before = right_paid = left_paid = None
        if s - LAG in got:
            over_even, over_odd = got[s - LAG]
            right_before, left_before = jnp.where(even, over_odd, over_even), jnp.where(even, over_even, over_odd)
            over_even, over_odd = paid[s - LAG]
            right_paid, left_paid = jnp.where(even, over_even, over_odd), jnp.where(even, over_odd, over_even)
        right = payload(s, position, right_before, left_paid)
        left = payload(s, mirrored, left_before, right_paid)
        return jnp.where(even, right, left), jnp.where(even, left, right)

    def finished(group):
        pieces = []
        for k in range(group * per_group, (group + 1) * per_group):
            chunk = None
            for r in range(half, planes):
                over_even, over_odd = paid[k + LAG * r]
                this = jnp.where(in_left == even, over_odd, over_even)
                chunk = this if chunk is None else jnp.where(far == r, this, chunk)
            pieces.append(chunk)
        whole = jnp.concatenate(pieces, axis=0).astype(jnp.float32)
        return lax.optimization_barrier((whole * (1.0 / scale)).astype(jnp.bfloat16))

    waiting = []
    for s in range(total_steps):
        if s - LAG in got:
            got[s - LAG], *_ = lax.optimization_barrier((got[s - LAG], paid[s - 1], *waiting))
            waiting = []
        paid[s] = payloads(s)
        links = ([], [])
        for i in range(hops):
            if 0 <= s - LAG * i < CHUNKS:
                links[i % 2].append((i, i + 1))
            if 0 <= s - LAG * (hops - 1 - i) < CHUNKS:
                links[i % 2].append((i + 1, i))
        if links[0] or links[1]:
            got[s] = tuple(
                lax.ppermute(p, "aux", pairs) if pairs else jnp.zeros_like(p) for p, pairs in zip(paid[s], links)
            )
        group, rest = divmod(s - LAG * hops + 1, per_group)
        if group > 0 and rest == 0:
            waiting.append(consume(group - 1, finished(group - 1)))
        waiting += at_step(total_steps - s)


def shards(tiles, slot_aux, slot_basis, slot_count, orbitals, fit_rows, *, groups, planes, across):
    position = lax.axis_index("aux")
    member = lax.axis_index("orb")
    slots, tile = tiles.shape[:2]
    aux_rows = fit_rows.shape[1]
    width = orbitals.shape[1]
    local_bases = orbitals.shape[0] // tile
    cap = min(slots, across * -(-7 * slots // (4 * planes * across)))
    part = cap // across
    later = -(-slots // cap) - 1

    live = jnp.arange(slots, dtype=jnp.int32)[None, :] < slot_count[:, None]
    target = jnp.where(live, slot_basis // local_bases, planes)
    plane_ids = jnp.arange(planes, dtype=jnp.int32)
    begins = jnp.sum(target[:, None, :] < plane_ids[None, :, None], axis=2, dtype=jnp.int32)
    counts = jnp.sum(target[:, None, :] == plane_ids[None, :, None], axis=2, dtype=jnp.int32)
    away = jnp.where(plane_ids[:, None] == plane_ids[None, :], 0, counts)
    rounds = (jnp.max(away) + cap - 1) // cap
    send_first = lax.dynamic_index_in_dim(begins, position, 0, keepdims=False)

    def exchange(turn):
        chosen = []
        for by in range(1, planes):
            first = send_first[(position + by) % planes] + turn * cap
            begin = jnp.minimum(first, slots - cap) + member * part
            chosen.append(lax.dynamic_slice_in_dim(tiles, begin, part, 0))
        return lax.optimization_barrier(chosen)

    def over_planes(chosen):
        return [lax.ppermute(c, "aux", rotation(planes, by)) for by, c in enumerate(chosen, 1)]

    def bound_of(largest):
        largest = jnp.broadcast_to(jnp.max(largest, axis=(1, 2))[:, None], (2, LANES))
        return [largest] + [lax.ppermute(largest, "aux", rotation(planes, by)) for by in range(1, planes)]

    chosen = exchange(jnp.int32(0))
    all_tiles, all_orbitals, rounds, _ = lax.optimization_barrier((tiles, orbitals, rounds, chosen))
    largest = largest_of(all_tiles, all_orbitals)
    most = rounds
    for by in range(1, groups):
        most = jnp.maximum(most, lax.ppermute(rounds, "groups", rotation(groups, by)))
    if planes == 4:
        first_hop = flipped(across, across // 2)
        sent, hopped = [lax.ppermute(chosen[0], "aux", rotation(planes, 1))], []
        later_tiles, sent[0], largest = lax.optimization_barrier((chosen[1], sent[0], largest))
        others = bound_of(largest)
        sent.append(lax.ppermute(later_tiles, "aux", rotation(planes, 2)))
        hopped.append(lax.ppermute(sent[0], "orb", first_hop))
        later_tiles, sent[1], hopped[0], others = lax.optimization_barrier((chosen[2], sent[1], hopped[0], others))
        sent.append(lax.ppermute(later_tiles, "aux", rotation(planes, 3)))
        hopped.append(lax.ppermute(sent[1], "orb", first_hop))
        sent[2], hopped[1], most = lax.optimization_barrier((sent[2], hopped[1], most))
        hopped.append(lax.ppermute(sent[2], "orb", first_hop))
        held = [over_members(a, "orb", across, {across // 2: h}) for a, h in zip(sent, hopped)]
        received = [h[e] for e in range(across) for h in held]
    else:
        others = bound_of(largest)
        received = over_members(jnp.concatenate(over_planes(chosen), axis=0), "orb", across)
    largest = functools.reduce(jnp.maximum, others)
    bound = tile * jnp.sum(counts).astype(jnp.float32) * largest[0, 0] * largest[1, 0]
    scale = 32768.0 / jnp.maximum(bound, 1e-30)

    def more(state):
        turn, kept = state
        arrived = jnp.concatenate(over_planes(exchange(turn)), axis=0)
        tiles_now = jnp.stack(over_members(arrived, "orb", across))
        return turn + 1, lax.dynamic_update_index_in_dim(kept, tiles_now, turn - 1, 0)

    batch = (planes - 1) * part
    empty = unfilled((max(later, 1), across, batch, tile, tile), tiles.dtype)
    _, overflow = lax.while_loop(lambda state: state[0] < most, more, (jnp.int32(1), empty))
    place = jnp.stack([position, member, most]).astype(jnp.int32)

    tables = (slot_aux, slot_basis, begins, counts)
    partial = spread(place, tables, tiles, received, overflow, orbitals, aux_rows, planes, across, cap)
    partial = partial.reshape(-1, LANES)
    column_groups = width // LANES
    fitted, wide = [], []
    square = planes == across
    blocks = {}

    def product(left, right):
        return jnp.einsum("pj,pi->ji", left, right, preferred_element_type=jnp.float32)

    def scatter(parts):
        stacked = jnp.stack(parts)

        def to(plane):
            return lax.dynamic_index_in_dim(stacked, plane ^ member, 0, keepdims=False)

        sent = [to((position + by) % planes).astype(jnp.bfloat16) for by in range(1, planes)]
        return [to(position)] + [lax.ppermute(t, "aux", rotation(planes, by)) for by, t in enumerate(sent, 1)], sent

    def total(terms):
        return sum((t.astype(jnp.float32) for t in terms[1:]), terms[0])

    def consume(g, rounded):
        last = g == column_groups - 1
        if square and last:
            rounded, _ = lax.optimization_barrier((rounded, blocks["corner_sent"]))
        own = jnp.dot(fit_rows, rounded, preferred_element_type=jnp.float32).astype(jnp.bfloat16)
        if square and last:
            blocks["upper"], _ = scatter([product(w, own) for w in blocks["early"]])
        fitted.append(own)
        if square:
            wide.append(over_members(own, "orb", across))
        if square and g == column_groups - 2:
            blocks["early"] = [jnp.concatenate([w[e] for w in wide], axis=1) for e in range(across)]
            inner = jnp.concatenate(fitted, axis=1)
            blocks["terms"] = [product(w, inner) for w in blocks["early"]]
        return own

    def at_step(steps_left):
        if "terms" in blocks and "corner" not in blocks and steps_left <= 3:
            blocks["corner"], blocks["corner_sent"] = scatter(blocks["terms"])
            return list(blocks["terms"])
        return []

    all_planes(partial, consume, at_step, column_groups, aux_rows, planes, position, scale)
    fitted = jnp.concatenate(fitted, axis=1)
    if square:
        lower = total(scatter([product(w, fitted) for w in wide[-1]])[0])
        upper = jnp.concatenate([total(blocks["corner"]), total(blocks["upper"])], axis=1)
        return jnp.concatenate([upper, lower], axis=0)
    wide = lax.all_gather(fitted, "orb", axis=1, tiled=True)
    return lax.psum_scatter(product(wide, fitted), "aux", scatter_dimension=0, tiled=True)


def solution(mesh):
    body = functools.partial(
        shards,
        groups=mesh.shape["groups"],
        planes=mesh.shape["aux"],
        across=mesh.shape["orb"],
    )
    return jax.shard_map(
        body,
        mesh=mesh,
        in_specs=(
            P(("groups", "aux"), None, None),
            P("groups", None),
            P("groups", None),
            P("groups"),
            P(("groups", "aux"), "orb"),
            P(("groups", "aux"), None),
        ),
        out_specs=P(("groups", "aux"), "orb"),
        check_vma=False,
    )
```

```python
import functools
import math

import jax
import jax.numpy as jnp
from jax import lax
from jax.experimental import pallas as pl
from jax.experimental.pallas import tpu as pltpu
from jax.sharding import PartitionSpec as P

LANES = 128
CHUNKS = 16
LAG = 2
UNROLL = 2


def rotation(size, by):
    return [(i, (i + by) % size) for i in range(size)]


def flipped(size, bit):
    return [(i, i ^ bit) for i in range(size)]


def over_members(array, axis, size, first=None):
    held = {0: array} | (first or {})
    bit = size // 4 if first else size // 2
    while bit:
        held |= {e | bit: lax.ppermute(a, axis, flipped(size, bit)) for e, a in held.items()}
        bit //= 2
    return [held[e] for e in range(size)]


def spread_kernel(planes, across, cap, place, table_aux, table_basis, begins, counts, own_tiles, *refs):
    received = refs[:-10]
    overflow, orbitals, sums, own, panels, held, chosen, owners, bases, arrived = refs[-10:]
    slots, tile = own_tiles.shape[:2]
    part = cap // across
    position, member, rounds = place[0], place[1], place[2]
    local_bases = panels.shape[0] // tile
    groups = sums.shape[0]

    early = [
        pltpu.make_async_copy(own_tiles, own, arrived.at[len(received)]),
        pltpu.make_async_copy(orbitals, panels, arrived.at[len(received) + 1]),
    ]
    for copy in early:
        copy.start()
    copies, at = [], 0
    for n, tiles in enumerate(received):
        copies.append(pltpu.make_async_copy(tiles, held.at[pl.ds(at, tiles.shape[0])], arrived.at[n]))
        at += tiles.shape[0]
    for copy in copies:
        copy.start()

    def clear(n, _):
        for g in range(groups):
            sums[g, pl.ds(pl.multiple_of(n * tile, tile), tile), :] = jnp.zeros((tile, LANES), jnp.float32)
        return 0

    lax.fori_loop(0, sums.shape[1] // tile, clear, 0)

    def rows_of(source, slot):
        return table_aux[source, slot] * tile, (table_basis[source, slot] - position * local_bases) * tile

    def ranges(turn, side, source):
        first = begins[source, position] + turn * cap
        last = jnp.minimum(first + cap, begins[source, position] + counts[source, position])
        begin = jnp.minimum(first, slots - cap) + side * part
        return begin, jnp.clip(first - begin, 0, part), jnp.clip(last - begin, 0, part)

    def term_of(block, base):
        panel = panels[pl.ds(pl.multiple_of(base, tile), tile), :]
        return jnp.dot(block, panel, preferred_element_type=jnp.float32)

    def add(owner, term):
        for g in range(groups):
            sums[g, pl.ds(pl.multiple_of(owner, tile), tile), :] += term[:, g * LANES : (g + 1) * LANES]

    def note_part(n, count):
        e, q = n // (planes - 1), lax.rem(n, planes - 1)
        source = lax.rem(position + (planes - 1 - q), planes)
        begin, low, high = ranges(0, member ^ e, source)

        def note(i, count):
            chosen[count] = n * part + i
            owners[count], bases[count] = rows_of(source, begin + i)
            return count + 1

        return lax.fori_loop(low, high, note, count)

    count = lax.fori_loop(0, across * (planes - 1), note_part, jnp.int32(0))
    for i in range(UNROLL - 1):
        chosen[count + i] = 0
        owners[count + i] = 0
        bases[count + i] = 0

    for copy in early:
        copy.wait()
    own_first = begins[position, position]
    own_count = counts[position, position]

    def several_own(n, _):
        terms = []
        for i in range(UNROLL):
            used = n * UNROLL + i < own_count
            slot = jnp.minimum(own_first + n * UNROLL + i, slots - 1)
            owner, base = rows_of(position, slot)
            term = term_of(own[slot], jnp.where(used, base, 0))
            terms.append((owner, jnp.where(used, term, 0.0)))
        for owner, term in terms:
            add(owner, term)
        return 0

    lax.fori_loop(0, (own_count + UNROLL - 1) // UNROLL, several_own, 0)
    for copy in copies:
        copy.wait()

    def several(n, _):
        terms = []
        for i in range(UNROLL):
            at = n * UNROLL + i
            term = term_of(held[chosen[at]], bases[at])
            terms.append((owners[at], jnp.where(at < count, term, 0.0)))
        for owner, term in terms:
            add(owner, term)
        return 0

    lax.fori_loop(0, (count + UNROLL - 1) // UNROLL, several, 0)

    def late_round(turn, _):
        def late_part(n, _):
            e, q = n // (planes - 1), lax.rem(n, planes - 1)
            source = lax.rem(position + (planes - 1 - q), planes)
            begin, low, high = ranges(turn, member ^ e, source)

            def late_one(i, _):
                pltpu.sync_copy(overflow.at[turn - 1, e, q * part + i], held.at[0])
                owner, base = rows_of(source, begin + i)
                add(owner, term_of(held[0], base))
                return 0

            return lax.fori_loop(low, high, late_one, 0)

        return lax.fori_loop(0, across * (planes - 1), late_part, 0)

    lax.fori_loop(1, rounds, late_round, 0)


def spread(place, tables, tiles, received, overflow, orbitals, rows, planes, across, cap):
    slots, tile = tiles.shape[:2]
    most = sum(r.shape[0] for r in received)
    smem = pl.BlockSpec(memory_space=pltpu.SMEM)
    vmem = pl.BlockSpec(memory_space=pltpu.VMEM)
    hbm = pl.BlockSpec(memory_space=pltpu.HBM)
    return pl.pallas_call(
        functools.partial(spread_kernel, planes, across, cap),
        out_shape=jax.ShapeDtypeStruct((orbitals.shape[1] // LANES, rows, LANES), jnp.float32),
        in_specs=[smem] * 5 + [hbm] * (1 + len(received) + 2),
        out_specs=vmem,
        scratch_shapes=[
            pltpu.VMEM(tiles.shape, tiles.dtype),
            pltpu.VMEM(orbitals.shape, orbitals.dtype),
            pltpu.VMEM((most, tile, tile), tiles.dtype),
            pltpu.SMEM((most + UNROLL,), jnp.int32),
            pltpu.SMEM((most + UNROLL,), jnp.int32),
            pltpu.SMEM((most + UNROLL,), jnp.int32),
            pltpu.SemaphoreType.DMA((len(received) + 2,)),
        ],
        compiler_params=pltpu.CompilerParams(vmem_limit_bytes=52 * 1024 * 1024),
        cost_estimate=pl.CostEstimate(
            flops=2 * slots * tile * tile * orbitals.shape[1],
            bytes_accessed=24 * 1024 * 1024,
            transcendentals=0,
        ),
    )(place, *tables, tiles, *received, overflow, orbitals)


def largest_kernel(steps, tiles, source, largest, panels, blocks, arrived):
    size = source.shape[0] // steps
    lanes = tiles.shape[-1]

    def piece(n):
        rows = pl.ds(n * size, size)
        return pltpu.make_async_copy(source.at[rows], panels.at[rows], arrived.at[n])

    whole = pltpu.make_async_copy(tiles, blocks, arrived.at[steps])
    whole.start()
    for n in range(steps):
        piece(n).start()
    whole.wait()

    def most_of_tile(n, most):
        return jnp.maximum(most, jnp.max(jnp.abs(blocks[n].reshape(-1, 16, lanes)), axis=0))

    most = lax.fori_loop(0, tiles.shape[0], most_of_tile, jnp.zeros((16, lanes), tiles.dtype))
    largest[0] = most.astype(jnp.float32)
    part = math.gcd(size, 240)

    def most_of_rows(n, most):
        block = panels[pl.ds(pl.multiple_of(n * part, part), part), :]
        return jnp.maximum(most, jnp.max(jnp.abs(block.reshape(-1, 16, source.shape[1])), axis=0))

    most = jnp.zeros((16, source.shape[1]), source.dtype)
    for n in range(steps):
        piece(n).wait()
        most = lax.fori_loop(n * (size // part), (n + 1) * (size // part), most_of_rows, most)
    across = most[:, :lanes]
    for g in range(1, source.shape[1] // lanes):
        across = jnp.maximum(across, most[:, g * lanes : (g + 1) * lanes])
    largest[1] = across.astype(jnp.float32)


def largest_of(tiles, orbitals):
    steps = 8
    hbm = pl.BlockSpec(memory_space=pltpu.HBM)
    return pl.pallas_call(
        functools.partial(largest_kernel, steps),
        out_shape=jax.ShapeDtypeStruct((2, 16, tiles.shape[-1]), jnp.float32),
        in_specs=[hbm, hbm],
        out_specs=pl.BlockSpec(memory_space=pltpu.VMEM),
        scratch_shapes=[
            pltpu.VMEM(orbitals.shape, orbitals.dtype),
            pltpu.VMEM(tiles.shape, tiles.dtype),
            pltpu.SemaphoreType.DMA((steps + 1,)),
        ],
        compiler_params=pltpu.CompilerParams(vmem_limit_bytes=52 * 1024 * 1024),
        cost_estimate=pl.CostEstimate(flops=0, bytes_accessed=10 * 1024 * 1024, transcendentals=0),
    )(tiles, orbitals)


def unfilled(shape, dtype):
    return pl.pallas_call(
        lambda out: None,
        out_shape=jax.ShapeDtypeStruct(shape, dtype),
        out_specs=pl.BlockSpec(memory_space=pltpu.HBM),
    )()


def all_planes(partial, consume, at_step, groups, rows, planes, position, scale):
    half = planes // 2
    per_group = CHUNKS // groups
    size = rows // per_group
    hops = planes - 1
    mirrored = hops - position
    in_left = position < half
    even = position % 2 == 0
    far = jnp.maximum(position, mirrored)
    got, paid = {}, {}
    total_steps = CHUNKS + LAG * hops

    def own_rows(s, rank):
        chunks = [s - LAG * r for r in range(half)]
        if not any(0 <= c < CHUNKS for c in chunks):
            return None
        at = jnp.clip(s - LAG * rank, 0, CHUNKS - 1) * size
        return lax.dynamic_slice_in_dim(partial, at, size, 0)

    def payload(s, rank, before, crossing):
        rows = own_rows(s, rank)
        total = None if rows is None else rows * scale
        if before is not None:
            crossing = jnp.where(rank == half, crossing.astype(jnp.float32), 0.0)
            added = crossing if total is None else jnp.where(rank < half, total, crossing)
            total = before.astype(jnp.float32) + added
        return total.astype(jnp.float16)

    def payloads(s):
        right_before = left_before = right_paid = left_paid = None
        if s - LAG in got:
            over_even, over_odd = got[s - LAG]
            right_before, left_before = jnp.where(even, over_odd, over_even), jnp.where(even, over_even, over_odd)
            over_even, over_odd = paid[s - LAG]
            right_paid, left_paid = jnp.where(even, over_even, over_odd), jnp.where(even, over_odd, over_even)
        right = payload(s, position, right_before, left_paid)
        left = payload(s, mirrored, left_before, right_paid)
        return jnp.where(even, right, left), jnp.where(even, left, right)

    def finished(first, last):
        pieces = []
        for k in range(first * per_group, last * per_group):
            chunk = None
            for r in range(half, planes):
                over_even, over_odd = paid[k + LAG * r]
                this = jnp.where(in_left == even, over_odd, over_even)
                chunk = this if chunk is None else jnp.where(far == r, this, chunk)
            pieces.append(chunk)
        whole = jnp.concatenate(pieces, axis=0).astype(jnp.float32)
        whole = (whole * (1.0 / scale)).astype(jnp.bfloat16)
        whole = [whole[g * rows : (g + 1) * rows] for g in range(last - first)]
        return lax.optimization_barrier(jnp.concatenate(whole, axis=1))

    waiting, taken = [], 0
    for s in range(total_steps):
        if s - LAG in got:
            got[s - LAG], *_ = lax.optimization_barrier((got[s - LAG], paid[s - 1], *waiting))
            waiting = []
        paid[s] = payloads(s)
        links = ([], [])
        for i in range(hops):
            if 0 <= s - LAG * i < CHUNKS:
                links[i % 2].append((i, i + 1))
            if 0 <= s - LAG * (hops - 1 - i) < CHUNKS:
                links[i % 2].append((i + 1, i))
        if links[0] or links[1]:
            got[s] = tuple(
                lax.ppermute(p, "aux", pairs) if pairs else jnp.zeros_like(p) for p, pairs in zip(paid[s], links)
            )
        group, rest = divmod(s - LAG * hops + 1, per_group)
        if rest == 0 and group > max(0, groups - 3):
            whole = finished(taken, group)
            waiting.append(consume(group == groups, whole))
            taken = group
        waiting += at_step(total_steps - s)


def shards(tiles, slot_aux, slot_basis, slot_count, orbitals, fit_rows, *, groups, planes, across):
    position = lax.axis_index("aux")
    member = lax.axis_index("orb")
    slots, tile = tiles.shape[:2]
    aux_rows = fit_rows.shape[1]
    width = orbitals.shape[1]
    local_bases = orbitals.shape[0] // tile
    cap = min(slots, across * -(-7 * slots // (4 * planes * across)))
    part = cap // across
    later = -(-slots // cap) - 1

    live = jnp.arange(slots, dtype=jnp.int32)[None, :] < slot_count[:, None]
    target = jnp.where(live, slot_basis // local_bases, planes)
    plane_ids = jnp.arange(planes, dtype=jnp.int32)
    begins = jnp.sum(target[:, None, :] < plane_ids[None, :, None], axis=2, dtype=jnp.int32)
    counts = jnp.sum(target[:, None, :] == plane_ids[None, :, None], axis=2, dtype=jnp.int32)
    away = jnp.where(plane_ids[:, None] == plane_ids[None, :], 0, counts)
    rounds = (jnp.max(away) + cap - 1) // cap
    send_first = lax.dynamic_index_in_dim(begins, position, 0, keepdims=False)

    def exchange(turn):
        chosen = []
        for by in range(1, planes):
            first = send_first[(position + by) % planes] + turn * cap
            begin = jnp.minimum(first, slots - cap) + member * part
            chosen.append(lax.dynamic_slice_in_dim(tiles, begin, part, 0))
        return lax.optimization_barrier(chosen)

    def over_planes(chosen):
        return [lax.ppermute(c, "aux", rotation(planes, by)) for by, c in enumerate(chosen, 1)]

    def bound_of(largest):
        largest = jnp.broadcast_to(jnp.max(largest, axis=(1, 2))[:, None], (2, LANES))
        return [largest] + [lax.ppermute(largest, "aux", rotation(planes, by)) for by in range(1, planes)]

    chosen = exchange(jnp.int32(0))
    all_tiles, all_orbitals, rounds, _ = lax.optimization_barrier((tiles, orbitals, rounds, chosen))
    largest = largest_of(all_tiles, all_orbitals)
    most = rounds
    for by in range(1, groups):
        most = jnp.maximum(most, lax.ppermute(rounds, "groups", rotation(groups, by)))
    if planes == 4:
        first_hop = flipped(across, across // 2)
        sent, hopped = [lax.ppermute(chosen[0], "aux", rotation(planes, 1))], []
        later_tiles, sent[0], largest = lax.optimization_barrier((chosen[1], sent[0], largest))
        others = bound_of(largest)
        sent.append(lax.ppermute(later_tiles, "aux", rotation(planes, 2)))
        hopped.append(lax.ppermute(sent[0], "orb", first_hop))
        later_tiles, sent[1], hopped[0], others = lax.optimization_barrier((chosen[2], sent[1], hopped[0], others))
        sent.append(lax.ppermute(later_tiles, "aux", rotation(planes, 3)))
        hopped.append(lax.ppermute(sent[1], "orb", first_hop))
        sent[2], hopped[1], most = lax.optimization_barrier((sent[2], hopped[1], most))
        hopped.append(lax.ppermute(sent[2], "orb", first_hop))
        held = [over_members(a, "orb", across, {across // 2: h}) for a, h in zip(sent, hopped)]
        received = [h[e] for e in range(across) for h in held]
    else:
        others = bound_of(largest)
        received = over_members(jnp.concatenate(over_planes(chosen), axis=0), "orb", across)
    largest = functools.reduce(jnp.maximum, others)
    bound = tile * jnp.sum(counts).astype(jnp.float32) * largest[0, 0] * largest[1, 0]
    scale = 32768.0 / jnp.maximum(bound, 1e-30)

    def more(state):
        turn, kept = state
        arrived = jnp.concatenate(over_planes(exchange(turn)), axis=0)
        tiles_now = jnp.stack(over_members(arrived, "orb", across))
        return turn + 1, lax.dynamic_update_index_in_dim(kept, tiles_now, turn - 1, 0)

    batch = (planes - 1) * part
    empty = unfilled((max(later, 1), across, batch, tile, tile), tiles.dtype)
    _, overflow = lax.while_loop(lambda state: state[0] < most, more, (jnp.int32(1), empty))
    place = jnp.stack([position, member, most]).astype(jnp.int32)

    tables = (slot_aux, slot_basis, begins, counts)
    partial = spread(place, tables, tiles, received, overflow, orbitals, aux_rows, planes, across, cap)
    partial = partial.reshape(-1, LANES)
    column_groups = width // LANES
    fitted, wide = [], []
    square = planes == across == 4
    blocks = {}

    def product(left, right):
        return jnp.einsum("pj,pi->ji", left, right, preferred_element_type=jnp.float32)

    def scatter(parts):
        stacked = jnp.stack(parts)

        def to(plane):
            return lax.dynamic_index_in_dim(stacked, plane ^ member, 0, keepdims=False)

        neighbour = position ^ 1
        sent = jnp.stack([to(neighbour), to(planes - 1 - neighbour)]).astype(jnp.bfloat16)
        near = lax.ppermute(sent, "aux", flipped(planes, 1))
        far = (to(planes - 1 - position) + near[1].astype(jnp.float32)).astype(jnp.bfloat16)
        return [to(position), near[0], lax.ppermute(far, "aux", flipped(planes, planes - 1))], sent

    def total(terms):
        return sum((t.astype(jnp.float32) for t in terms[1:]), terms[0])

    def consume(last, rounded):
        if square and last:
            rounded, _ = lax.optimization_barrier((rounded, blocks["corner_sent"]))
        own = jnp.dot(fit_rows, rounded, preferred_element_type=jnp.float32).astype(jnp.bfloat16)
        if square and last:
            blocks["upper"], _ = scatter([product(w, own) for w in blocks["early"]])
        fitted.append(own)
        if square:
            wide.append(over_members(own, "orb", across))
        if square and not last and len(fitted) == 2:
            blocks["early"] = [jnp.concatenate([w[e] for w in wide], axis=1) for e in range(across)]
            inner = jnp.concatenate(fitted, axis=1)
            blocks["terms"] = [product(w, inner) for w in blocks["early"]]
        return own

    def at_step(steps_left):
        if "terms" in blocks and "corner" not in blocks and steps_left <= 3:
            blocks["corner"], blocks["corner_sent"] = scatter(blocks["terms"])
            return list(blocks["terms"])
        return []

    all_planes(partial, consume, at_step, column_groups, aux_rows, planes, position, scale)
    fitted = jnp.concatenate(fitted, axis=1)
    if square:
        lower = total(scatter([product(w, fitted) for w in wide[-1]])[0])
        upper = jnp.concatenate([total(blocks["corner"]), total(blocks["upper"])], axis=1)
        return jnp.concatenate([upper, lower], axis=0)
    wide = lax.all_gather(fitted, "orb", axis=1, tiled=True)
    return lax.psum_scatter(product(wide, fitted), "aux", scatter_dimension=0, tiled=True)


def solution(mesh):
    body = functools.partial(
        shards,
        groups=mesh.shape["groups"],
        planes=mesh.shape["aux"],
        across=mesh.shape["orb"],
    )
    return jax.shard_map(
        body,
        mesh=mesh,
        in_specs=(
            P(("groups", "aux"), None, None),
            P("groups", None),
            P("groups", None),
            P("groups"),
            P(("groups", "aux"), "orb"),
            P(("groups", "aux"), None),
        ),
        out_specs=P(("groups", "aux"), "orb"),
        check_vma=False,
    )
```

```python
import functools
import math

import jax
import jax.numpy as jnp
from jax import lax
from jax.experimental import pallas as pl
from jax.experimental.pallas import tpu as pltpu
from jax.sharding import PartitionSpec as P

LANES = 128
CHUNKS = 16
LAG = 2
UNROLL = 2


def rotation(size, by):
    return [(i, (i + by) % size) for i in range(size)]


def flipped(size, bit):
    return [(i, i ^ bit) for i in range(size)]


def over_members(array, axis, size, first=None):
    held = {0: array} | (first or {})
    bit = size // 4 if first else size // 2
    while bit:
        held |= {e | bit: lax.ppermute(a, axis, flipped(size, bit)) for e, a in held.items()}
        bit //= 2
    return [held[e] for e in range(size)]


def spread_kernel(planes, across, cap, place, table_aux, table_basis, begins, counts, own_tiles, *refs):
    received = refs[:-10]
    overflow, orbitals, sums, own, panels, held, chosen, owners, bases, arrived = refs[-10:]
    slots, tile = own_tiles.shape[:2]
    part = cap // across
    position, member, rounds = place[0], place[1], place[2]
    local_bases = panels.shape[0] // tile
    groups = sums.shape[0]

    early = [
        pltpu.make_async_copy(own_tiles, own, arrived.at[len(received)]),
        pltpu.make_async_copy(orbitals, panels, arrived.at[len(received) + 1]),
    ]
    for copy in early:
        copy.start()
    copies, at = [], 0
    for n, tiles in enumerate(received):
        copies.append(pltpu.make_async_copy(tiles, held.at[pl.ds(at, tiles.shape[0])], arrived.at[n]))
        at += tiles.shape[0]
    for copy in copies:
        copy.start()

    def clear(n, _):
        for g in range(groups):
            sums[g, pl.ds(pl.multiple_of(n * tile, tile), tile), :] = jnp.zeros((tile, LANES), jnp.float32)
        return 0

    lax.fori_loop(0, sums.shape[1] // tile, clear, 0)

    def rows_of(source, slot):
        return table_aux[source, slot] * tile, (table_basis[source, slot] - position * local_bases) * tile

    def ranges(turn, side, source):
        first = begins[source, position] + turn * cap
        last = jnp.minimum(first + cap, begins[source, position] + counts[source, position])
        begin = jnp.minimum(first, slots - cap) + side * part
        return begin, jnp.clip(first - begin, 0, part), jnp.clip(last - begin, 0, part)

    def term_of(block, base):
        panel = panels[pl.ds(pl.multiple_of(base, tile), tile), :]
        return jnp.dot(block, panel, preferred_element_type=jnp.float32)

    def add(owner, term):
        for g in range(groups):
            sums[g, pl.ds(pl.multiple_of(owner, tile), tile), :] += term[:, g * LANES : (g + 1) * LANES]

    def note_part(n, count):
        e, q = n // (planes - 1), lax.rem(n, planes - 1)
        source = lax.rem(position + (planes - 1 - q), planes)
        begin, low, high = ranges(0, member ^ e, source)

        def note(i, count):
            chosen[count] = n * part + i
            owners[count], bases[count] = rows_of(source, begin + i)
            return count + 1

        return lax.fori_loop(low, high, note, count)

    count = lax.fori_loop(0, across * (planes - 1), note_part, jnp.int32(0))
    for i in range(UNROLL - 1):
        chosen[count + i] = 0
        owners[count + i] = 0
        bases[count + i] = 0

    for copy in early:
        copy.wait()
    own_first = begins[position, position]
    own_count = counts[position, position]

    def several_own(n, _):
        terms = []
        for i in range(UNROLL):
            used = n * UNROLL + i < own_count
            slot = jnp.minimum(own_first + n * UNROLL + i, slots - 1)
            owner, base = rows_of(position, slot)
            term = term_of(own[slot], jnp.where(used, base, 0))
            terms.append((owner, jnp.where(used, term, 0.0)))
        for owner, term in terms:
            add(owner, term)
        return 0

    lax.fori_loop(0, (own_count + UNROLL - 1) // UNROLL, several_own, 0)
    for copy in copies:
        copy.wait()

    def several(n, _):
        terms = []
        for i in range(UNROLL):
            at = n * UNROLL + i
            term = term_of(held[chosen[at]], bases[at])
            terms.append((owners[at], jnp.where(at < count, term, 0.0)))
        for owner, term in terms:
            add(owner, term)
        return 0

    lax.fori_loop(0, (count + UNROLL - 1) // UNROLL, several, 0)

    def late_round(turn, _):
        def late_part(n, _):
            e, q = n // (planes - 1), lax.rem(n, planes - 1)
            source = lax.rem(position + (planes - 1 - q), planes)
            begin, low, high = ranges(turn, member ^ e, source)

            def late_one(i, _):
                pltpu.sync_copy(overflow.at[turn - 1, e, q * part + i], held.at[0])
                owner, base = rows_of(source, begin + i)
                add(owner, term_of(held[0], base))
                return 0

            return lax.fori_loop(low, high, late_one, 0)

        return lax.fori_loop(0, across * (planes - 1), late_part, 0)

    lax.fori_loop(1, rounds, late_round, 0)


def spread(place, tables, tiles, received, overflow, orbitals, rows, planes, across, cap):
    slots, tile = tiles.shape[:2]
    most = sum(r.shape[0] for r in received)
    smem = pl.BlockSpec(memory_space=pltpu.SMEM)
    vmem = pl.BlockSpec(memory_space=pltpu.VMEM)
    hbm = pl.BlockSpec(memory_space=pltpu.HBM)
    return pl.pallas_call(
        functools.partial(spread_kernel, planes, across, cap),
        out_shape=jax.ShapeDtypeStruct((orbitals.shape[1] // LANES, rows, LANES), jnp.float32),
        in_specs=[smem] * 5 + [hbm] * (1 + len(received) + 2),
        out_specs=vmem,
        scratch_shapes=[
            pltpu.VMEM(tiles.shape, tiles.dtype),
            pltpu.VMEM(orbitals.shape, orbitals.dtype),
            pltpu.VMEM((most, tile, tile), tiles.dtype),
            pltpu.SMEM((most + UNROLL,), jnp.int32),
            pltpu.SMEM((most + UNROLL,), jnp.int32),
            pltpu.SMEM((most + UNROLL,), jnp.int32),
            pltpu.SemaphoreType.DMA((len(received) + 2,)),
        ],
        compiler_params=pltpu.CompilerParams(vmem_limit_bytes=52 * 1024 * 1024),
        cost_estimate=pl.CostEstimate(
            flops=2 * slots * tile * tile * orbitals.shape[1],
            bytes_accessed=24 * 1024 * 1024,
            transcendentals=0,
        ),
    )(place, *tables, tiles, *received, overflow, orbitals)


def largest_kernel(steps, tiles, source, largest, panels, blocks, arrived):
    size = source.shape[0] // steps
    lanes = tiles.shape[-1]

    def piece(n):
        rows = pl.ds(n * size, size)
        return pltpu.make_async_copy(source.at[rows], panels.at[rows], arrived.at[n])

    whole = pltpu.make_async_copy(tiles, blocks, arrived.at[steps])
    whole.start()
    for n in range(steps):
        piece(n).start()
    whole.wait()

    def most_of_tile(n, most):
        return jnp.maximum(most, jnp.max(jnp.abs(blocks[n].reshape(-1, 16, lanes)), axis=0))

    most = lax.fori_loop(0, tiles.shape[0], most_of_tile, jnp.zeros((16, lanes), tiles.dtype))
    largest[0] = most.astype(jnp.float32)
    part = math.gcd(size, 240)

    def most_of_rows(n, most):
        block = panels[pl.ds(pl.multiple_of(n * part, part), part), :]
        return jnp.maximum(most, jnp.max(jnp.abs(block.reshape(-1, 16, source.shape[1])), axis=0))

    most = jnp.zeros((16, source.shape[1]), source.dtype)
    for n in range(steps):
        piece(n).wait()
        most = lax.fori_loop(n * (size // part), (n + 1) * (size // part), most_of_rows, most)
    across = most[:, :lanes]
    for g in range(1, source.shape[1] // lanes):
        across = jnp.maximum(across, most[:, g * lanes : (g + 1) * lanes])
    largest[1] = across.astype(jnp.float32)


def largest_of(tiles, orbitals):
    steps = 8
    hbm = pl.BlockSpec(memory_space=pltpu.HBM)
    return pl.pallas_call(
        functools.partial(largest_kernel, steps),
        out_shape=jax.ShapeDtypeStruct((2, 16, tiles.shape[-1]), jnp.float32),
        in_specs=[hbm, hbm],
        out_specs=pl.BlockSpec(memory_space=pltpu.VMEM),
        scratch_shapes=[
            pltpu.VMEM(orbitals.shape, orbitals.dtype),
            pltpu.VMEM(tiles.shape, tiles.dtype),
            pltpu.SemaphoreType.DMA((steps + 1,)),
        ],
        compiler_params=pltpu.CompilerParams(vmem_limit_bytes=52 * 1024 * 1024),
        cost_estimate=pl.CostEstimate(flops=0, bytes_accessed=10 * 1024 * 1024, transcendentals=0),
    )(tiles, orbitals)


def unfilled(shape, dtype):
    return pl.pallas_call(
        lambda out: None,
        out_shape=jax.ShapeDtypeStruct(shape, dtype),
        out_specs=pl.BlockSpec(memory_space=pltpu.HBM),
    )()


def all_planes(partial, consume, at_step, groups, rows, planes, position, scale):
    half = planes // 2
    per_group = CHUNKS // groups
    size = rows // per_group
    hops = planes - 1
    mirrored = hops - position
    in_left = position < half
    even = position % 2 == 0
    far = jnp.maximum(position, mirrored)
    got, paid = {}, {}
    total_steps = CHUNKS + LAG * hops

    def own_rows(s, rank):
        chunks = [s - LAG * r for r in range(half)]
        if not any(0 <= c < CHUNKS for c in chunks):
            return None
        at = jnp.clip(s - LAG * rank, 0, CHUNKS - 1) * size
        return lax.dynamic_slice_in_dim(partial, at, size, 0)

    def payload(s, rank, before, crossing):
        rows = own_rows(s, rank)
        total = None if rows is None else rows * scale
        if before is not None:
            crossing = jnp.where(rank == half, crossing.astype(jnp.float32), 0.0)
            added = crossing if total is None else jnp.where(rank < half, total, crossing)
            total = before.astype(jnp.float32) + added
        return total.astype(jnp.float16)

    def payloads(s):
        right_before = left_before = right_paid = left_paid = None
        if s - LAG in got:
            over_even, over_odd = got[s - LAG]
            right_before, left_before = jnp.where(even, over_odd, over_even), jnp.where(even, over_even, over_odd)
            over_even, over_odd = paid[s - LAG]
            right_paid, left_paid = jnp.where(even, over_even, over_odd), jnp.where(even, over_odd, over_even)
        right = payload(s, position, right_before, left_paid)
        left = payload(s, mirrored, left_before, right_paid)
        return jnp.where(even, right, left), jnp.where(even, left, right)

    def finished(first, last):
        pieces = []
        for k in range(first * per_group, last * per_group):
            chunk = None
            for r in range(half, planes):
                over_even, over_odd = paid[k + LAG * r]
                this = jnp.where(in_left == even, over_odd, over_even)
                chunk = this if chunk is None else jnp.where(far == r, this, chunk)
            pieces.append(chunk)
        whole = jnp.concatenate(pieces, axis=0).astype(jnp.float32)
        whole = (whole * (1.0 / scale)).astype(jnp.bfloat16)
        whole = [whole[g * rows : (g + 1) * rows] for g in range(last - first)]
        return lax.optimization_barrier(jnp.concatenate(whole, axis=1))

    waiting, taken = [], 0
    for s in range(total_steps):
        if s - LAG in got:
            got[s - LAG], *_ = lax.optimization_barrier((got[s - LAG], paid[s - 1], *waiting))
            waiting = []
        paid[s] = payloads(s)
        links = ([], [])
        for i in range(hops):
            if 0 <= s - LAG * i < CHUNKS:
                links[i % 2].append((i, i + 1))
            if 0 <= s - LAG * (hops - 1 - i) < CHUNKS:
                links[i % 2].append((i + 1, i))
        if links[0] or links[1]:
            got[s] = tuple(
                lax.ppermute(p, "aux", pairs) if pairs else jnp.zeros_like(p) for p, pairs in zip(paid[s], links)
            )
        group, rest = divmod(s - LAG * hops + 1, per_group)
        if rest == 0 and group > max(0, groups - 3):
            whole = finished(taken, group)
            waiting.append(consume(group == groups, whole))
            taken = group
        waiting += at_step(total_steps - s)


def shards(tiles, slot_aux, slot_basis, slot_count, orbitals, fit_rows, *, groups, planes, across):
    position = lax.axis_index("aux")
    member = lax.axis_index("orb")
    slots, tile = tiles.shape[:2]
    aux_rows = fit_rows.shape[1]
    width = orbitals.shape[1]
    local_bases = orbitals.shape[0] // tile
    cap = min(slots, across * -(-7 * slots // (4 * planes * across)))
    part = cap // across
    later = -(-slots // cap) - 1

    live = jnp.arange(slots, dtype=jnp.int32)[None, :] < slot_count[:, None]
    target = jnp.where(live, slot_basis // local_bases, planes)
    plane_ids = jnp.arange(planes, dtype=jnp.int32)
    begins = jnp.sum(target[:, None, :] < plane_ids[None, :, None], axis=2, dtype=jnp.int32)
    counts = jnp.sum(target[:, None, :] == plane_ids[None, :, None], axis=2, dtype=jnp.int32)
    away = jnp.where(plane_ids[:, None] == plane_ids[None, :], 0, counts)
    rounds = (jnp.max(away) + cap - 1) // cap
    send_first = lax.dynamic_index_in_dim(begins, position, 0, keepdims=False)

    def exchange(turn):
        chosen = []
        for by in range(1, planes):
            first = send_first[(position + by) % planes] + turn * cap
            begin = jnp.minimum(first, slots - cap) + member * part
            chosen.append(lax.dynamic_slice_in_dim(tiles, begin, part, 0))
        return lax.optimization_barrier(chosen)

    def over_planes(chosen):
        return [lax.ppermute(c, "aux", rotation(planes, by)) for by, c in enumerate(chosen, 1)]

    def bound_of(largest):
        largest = jnp.broadcast_to(jnp.max(largest, axis=(1, 2))[:, None], (2, LANES))
        return [largest] + [lax.ppermute(largest, "aux", rotation(planes, by)) for by in range(1, planes)]

    chosen = exchange(jnp.int32(0))
    all_tiles, all_orbitals, rounds, _ = lax.optimization_barrier((tiles, orbitals, rounds, chosen))
    largest = largest_of(all_tiles, all_orbitals)
    most = rounds
    for by in range(1, groups):
        most = jnp.maximum(most, lax.ppermute(rounds, "groups", rotation(groups, by)))
    if planes == 4:
        first_hop = flipped(across, across // 2)
        sent, hopped = [lax.ppermute(chosen[0], "aux", rotation(planes, 1))], []
        later_tiles, sent[0], largest = lax.optimization_barrier((chosen[1], sent[0], largest))
        others = bound_of(largest)
        sent.append(lax.ppermute(later_tiles, "aux", rotation(planes, 2)))
        hopped.append(lax.ppermute(sent[0], "orb", first_hop))
        later_tiles, sent[1], hopped[0], others = lax.optimization_barrier((chosen[2], sent[1], hopped[0], others))
        sent.append(lax.ppermute(later_tiles, "aux", rotation(planes, 3)))
        hopped.append(lax.ppermute(sent[1], "orb", first_hop))
        sent[2], hopped[1], most = lax.optimization_barrier((sent[2], hopped[1], most))
        hopped.append(lax.ppermute(sent[2], "orb", first_hop))
        held = [over_members(a, "orb", across, {across // 2: h}) for a, h in zip(sent, hopped)]
        received = [h[e] for e in range(across) for h in held]
    else:
        others = bound_of(largest)
        received = over_members(jnp.concatenate(over_planes(chosen), axis=0), "orb", across)
    largest = functools.reduce(jnp.maximum, others)
    bound = tile * jnp.sum(counts).astype(jnp.float32) * largest[0, 0] * largest[1, 0]
    scale = 32768.0 / jnp.maximum(bound, 1e-30)

    def more(state):
        turn, kept = state
        arrived = jnp.concatenate(over_planes(exchange(turn)), axis=0)
        tiles_now = jnp.stack(over_members(arrived, "orb", across))
        return turn + 1, lax.dynamic_update_index_in_dim(kept, tiles_now, turn - 1, 0)

    batch = (planes - 1) * part
    empty = unfilled((max(later, 1), across, batch, tile, tile), tiles.dtype)
    _, overflow = lax.while_loop(lambda state: state[0] < most, more, (jnp.int32(1), empty))
    place = jnp.stack([position, member, most]).astype(jnp.int32)

    tables = (slot_aux, slot_basis, begins, counts)
    partial = spread(place, tables, tiles, received, overflow, orbitals, aux_rows, planes, across, cap)
    partial = partial.reshape(-1, LANES)
    column_groups = width // LANES
    fitted, wide = [], []
    square = planes == across == 4
    blocks = {}

    def product(left, right):
        return jnp.einsum("pj,pi->ji", left, right, preferred_element_type=jnp.float32)

    def scatter(parts):
        stacked = jnp.stack(parts)

        def to(plane):
            return lax.dynamic_index_in_dim(stacked, plane ^ member, 0, keepdims=False)

        neighbour = position ^ 1
        sent = jnp.stack([to(neighbour), to(planes - 1 - neighbour)]).astype(jnp.bfloat16)
        near = lax.ppermute(sent, "aux", flipped(planes, 1))
        far = (to(planes - 1 - position) + near[1].astype(jnp.float32)).astype(jnp.bfloat16)
        return [to(position), near[0], lax.ppermute(far, "aux", flipped(planes, planes - 1))], sent

    def total(terms):
        return sum((t.astype(jnp.float32) for t in terms[1:]), terms[0])

    def consume(last, rounded):
        if square and last:
            rounded, _ = lax.optimization_barrier((rounded, blocks["corner_sent"]))
        own = jnp.dot(fit_rows, rounded, preferred_element_type=jnp.float32).astype(jnp.bfloat16)
        if square and last:
            blocks["upper"], _ = scatter([product(w, own) for w in blocks["early"]])
        fitted.append(own)
        if square:
            wide.append(over_members(own, "orb", across))
        if square and not last and len(fitted) == 2:
            blocks["early"] = [jnp.concatenate([w[e] for w in wide], axis=1) for e in range(across)]
            inner = jnp.concatenate(fitted, axis=1)
            blocks["terms"] = [product(w, inner) for w in blocks["early"]]
        return own

    def at_step(steps_left):
        if "terms" in blocks and "corner" not in blocks and steps_left <= 4:
            blocks["corner"], blocks["corner_sent"] = scatter(blocks["terms"])
            return list(blocks["terms"])
        return []

    all_planes(partial, consume, at_step, column_groups, aux_rows, planes, position, scale)
    fitted = jnp.concatenate(fitted, axis=1)
    if square:
        lower = total(scatter([product(w, fitted) for w in wide[-1]])[0])
        upper = jnp.concatenate([total(blocks["corner"]), total(blocks["upper"])], axis=1)
        return jnp.concatenate([upper, lower], axis=0)
    wide = lax.all_gather(fitted, "orb", axis=1, tiled=True)
    return lax.psum_scatter(product(wide, fitted), "aux", scatter_dimension=0, tiled=True)


def solution(mesh):
    body = functools.partial(
        shards,
        groups=mesh.shape["groups"],
        planes=mesh.shape["aux"],
        across=mesh.shape["orb"],
    )
    return jax.shard_map(
        body,
        mesh=mesh,
        in_specs=(
            P(("groups", "aux"), None, None),
            P("groups", None),
            P("groups", None),
            P("groups"),
            P(("groups", "aux"), "orb"),
            P(("groups", "aux"), None),
        ),
        out_specs=P(("groups", "aux"), "orb"),
        check_vma=False,
    )
```
